128 devices in a mesh: tx: 8 (over z, core), ty: 16 (over x, y).
Axes of the slice: x: 4, y: 4, z: 4, core: 2. Of those that a mesh axis runs over, the one named last changes fastest.
Arguments:
- voxels: bfloat16 [524288, 128], P(('tx', 'ty')), may hold values from 0 to 9
- owner_tile: int32 [524288, 1], P(('tx', 'ty')), may hold values from 0 to 127; in each aligned block of 4096 rows (0 to 4095, 4096 to 8191, ...) at most 64 rows name the same one
- rim_blocks: int32 [128, 4, 16], P(('tx', 'ty')), may hold values from 0 to 127
- kernel_map: int32 [128, 27, 8192], P(('tx', 'ty')), may hold values from -1 to 12287, as said below
- weights: bfloat16 [27, 128, 128], replicated, may hold values from -0.109375 to 0.109375
- norm_gain: float32 [128], replicated, may hold values from 0.1 to 1.9
- shift_bias: float32 [128], replicated, may hold values from -3 to 3
Outputs:
- normalized: bfloat16 [1048576, 128], P(('tx', 'ty'))
The draws below stay inside these ranges and needn't reach their ends.
Inputs may be any that keep to these rules, and one draw needn't show every extreme that they name: `owner_tile`: at most 64 of one device's 4096 rows name one tile, and in every draw some device's rows name some tile exactly 64 times. `kernel_map`: for each tile, offset and aligned block of 64 output slots, all entries other than -1 lie in one block of the extended rows. The middle offset maps every slot to itself.
All inputs are finite; a program needn't handle non-finite values.
Results may differ from the reference program's by a relative error of at most 0.0004.
Values may be sent and summed in bfloat16 or wider, within the bound.
No kernel may reach another device: no remote copies, remote signals or barrier semaphores. Data moves between devices by JAX's collectives and lax.ppermute only.
A program may use at most 64 MiB of HBM per device.

```python
import math
import jax
import jax.numpy as jnp
import numpy as np
from jax import lax

C_IN = 128
C_OUT = 128
OFFSETS = 27
BLOCK = 64
HB = 16
SRC_ROWS = 4096
TILES = 128
GRID_ROWS = 8
GRID_COLS = 16
PAIR_ROWS = 64
TILE_BLOCKS = 128
TILE_ROWS = 8192
EXT_BLOCKS = 192
TOTAL = 524288


def draw_voxels(key, part):
    key = jax.random.fold_in(key, 11)
    subkeys = jax.random.split(key, 3)
    base = jax.random.normal(subkeys[0], (TOTAL, C_IN), jnp.float32)
    feature = jnp.clip(base, 0.0, 6.0)
    offset = jax.random.uniform(subkeys[2], (1, C_IN), jnp.float32, 0.0, 0.5)
    return (feature + offset).astype(jnp.bfloat16)


def draw_kernel_map(key, part):
    key = jax.random.fold_in(key, 7)
    subkeys = jax.random.split(key, 4)
    block_shape = (TILES, OFFSETS, TILE_BLOCKS)
    slot_shape = (TILES, OFFSETS, TILE_BLOCKS, BLOCK)
    source_block = jax.random.randint(subkeys[0], block_shape, 0, EXT_BLOCKS)
    chance = jax.random.randint(subkeys[1], block_shape, 0, 1000)
    density = 250 + 500 * jnp.arange(TILES, dtype=jnp.int32) // max(TILES - 1, 1)
    present = chance < density[:, None, None]
    within = jax.random.randint(subkeys[2], slot_shape, 0, BLOCK)
    missing = jax.random.randint(subkeys[3], slot_shape, 0, 4) == 0
    mapped = source_block[..., None] * BLOCK + within
    mapped = jnp.where(present[..., None] & jnp.logical_not(missing), mapped, -1)
    centre = jnp.arange(TILE_ROWS, dtype=jnp.int32).reshape(1, TILE_BLOCKS, BLOCK)
    mapped = mapped.at[:, OFFSETS // 2].set(jnp.broadcast_to(centre, (TILES, TILE_BLOCKS, BLOCK)))
    return mapped.reshape(TILES, OFFSETS, TILE_ROWS).astype(jnp.int32)


def place_ends(drawn, stream_key, least, high):
    dims = drawn.shape
    place = [jax.random.randint(jax.random.fold_in(stream_key, axis), (), 0, dims[axis]) for axis in range(len(dims))]
    drawn = drawn.at[tuple(place)].set(least)
    longest = dims.index(max(dims))
    place[longest] = (place[longest] + 1) % dims[longest]
    return drawn.at[tuple(place)].set(high)


def shared_out(rng, own, number, rows, amount, top, reach, skew):
    ranking = jax.random.permutation(rng, amount)
    heavy_load, common = shares(amount, rows * top, reach, skew, True), shares(amount, rows * top, reach, skew, False)
    places = jnp.arange(amount)

    def named(lengths, turn):
        used = int((lengths > 0).sum())
        fixed = max(1, used // 4)
        shifted = fixed + (places - fixed + turn * (used - fixed)) % max(1, amount - fixed)
        return jnp.zeros((amount,), jnp.int32).at[ranking[jnp.where(places < fixed, places, shifted)]].set(jnp.asarray(lengths, jnp.int32))

    lengths = jnp.where(number % 4 == 0, named(heavy_load, number // 4), named(common, number - number // 4 - 1))
    mixed = jax.random.permutation(jax.random.fold_in(own, 3), amount)
    giver, receiver = mixed[0:amount // 2 * 2:2], mixed[1:amount // 2 * 2:2]
    room = jnp.minimum(lengths[giver] - 1, reach - lengths[receiver]) // 2
    room = jnp.where((giver == ranking[0]) | (receiver == ranking[0]) | (lengths[receiver] == 0), 0, jnp.maximum(room, 0))
    shifted = jax.random.randint(jax.random.fold_in(own, 4), (amount // 2,), 0, 1 << 20) % (room + 1)
    lengths = lengths.at[giver].add(-shifted).at[receiver].add(shifted)
    members = jnp.searchsorted(jnp.cumsum(lengths), jnp.arange(rows * top), side="right").astype(jnp.int32)
    table = members.reshape(top, rows).T
    table = table[jax.random.permutation(jax.random.fold_in(own, 1), rows)]
    turn = jax.random.randint(jax.random.fold_in(own, 2), (rows, 1), 0, top)
    return jnp.take_along_axis(table, (jnp.arange(top)[None, :] + turn) % top, axis=1)


def shares(amount, total, bound, slope, full):
    portions = [(1 << 20) // math.isqrt(standing ** slope) + 1 for standing in range(1, amount + 1)]
    largest = bound if full else min(bound, max(-(-total // amount), total * portions[0] // sum(portions)))
    least = 1 if total - largest >= amount - 1 else 0
    given, spare = [largest] + [least] * (amount - 1), total - largest - least * (amount - 1)
    while spare > 0:
        free = [i for i in range(1, amount) if given[i] < largest] or [i for i in range(1, amount) if given[i] < bound]
        pool, budget = sum([portions[i] for i in free]), spare
        for i in free:
            addition = min(bound - given[i], max(1, budget * portions[i] // pool), spare)
            given[i] = given[i] + addition
            spare = spare - addition
    return np.array(given)


def noise(stream_key, extent, deviation, bound, held_as=jnp.bfloat16):
    return jnp.clip(deviation * jax.random.normal(stream_key, extent, jnp.float32), -bound, bound).astype(held_as)


def setup_inputs(seed: int = 0) -> dict:
    streams_of = jax.random.split(jax.random.key(seed), 8)
    voxels = draw_voxels(jax.random.fold_in(streams_of[7], 71), 0)
    owner_tile_keys = jax.random.split(jax.random.fold_in(streams_of[1], 1), TOTAL // SRC_ROWS)
    owner_tile_turns = jax.random.permutation(jax.random.fold_in(streams_of[1], 3), TOTAL // SRC_ROWS)
    owner_tile = jax.vmap(lambda own, number: shared_out(jax.random.fold_in(streams_of[1], 2), own, number, SRC_ROWS, TILES, 1, PAIR_ROWS, 1))(owner_tile_keys, owner_tile_turns).reshape((TOTAL, 1))
    rim_blocks = place_ends(jax.random.randint(streams_of[2], (TILES, 4, HB), 0, TILE_BLOCKS), jax.random.fold_in(streams_of[2], 1), 0, TILE_BLOCKS - 1).astype(jnp.int32)
    kernel_map = draw_kernel_map(jax.random.fold_in(streams_of[7], 71), 0)
    weights = noise(streams_of[4], (OFFSETS, C_IN, C_OUT), (OFFSETS * C_IN) ** -0.5, 0.109375)
    norm_gain = jnp.clip(1.0 + 0.18 * jax.random.normal(streams_of[5], (C_OUT,), jnp.float32), 0.1, 1.9)
    shift_bias = noise(streams_of[6], (C_OUT,), 0.5, 3.0, jnp.float32)
    return {"voxels": voxels, "owner_tile": owner_tile, "rim_blocks": rim_blocks, "kernel_map": kernel_map, "weights": weights, "norm_gain": norm_gain, "shift_bias": shift_bias}


def route_one(bundle):
    payload, targets = bundle
    onehot = (targets[:, None] == jnp.arange(TILES, dtype=jnp.int32)[None, :]).astype(jnp.int32)
    placed = lax.optimization_barrier(jnp.sum((jnp.cumsum(onehot, axis=0) - 1) * onehot, axis=1)).astype(jnp.int32)
    address = (targets * PAIR_ROWS + placed).astype(jnp.int32)
    outgoing = jnp.zeros((TILES * PAIR_ROWS, C_IN), payload.dtype).at[address].set(payload)
    filled = lax.optimization_barrier(jnp.sum(onehot, axis=0)).astype(jnp.int32)
    return (outgoing.reshape(TILES, PAIR_ROWS, C_IN), filled)

def reference(voxels, owner_tile, rim_blocks, kernel_map, weights, norm_gain, shift_bias):
    outgoing, filled = lax.map(route_one, (voxels.reshape(TILES, SRC_ROWS, C_IN), owner_tile.reshape(TILES, SRC_ROWS)))
    arrival = jnp.swapaxes(outgoing, 0, 1).reshape(TILES, TILE_ROWS, C_IN)
    occupied = jnp.arange(PAIR_ROWS, dtype=jnp.int32)[None, None, :] < jnp.swapaxes(filled, 0, 1)[:, :, None]
    occupied = occupied.astype(jnp.float32).reshape(TILES, TILE_ROWS)
    blocked = arrival.reshape(TILES, TILE_BLOCKS, BLOCK, C_IN)
    weights_wide = weights.astype(jnp.float32)

    def one_tile(tile_index):
        grid_row = tile_index // GRID_COLS
        grid_col = tile_index % GRID_COLS
        pieces = [arrival[tile_index]]
        sources = ((tile_index - GRID_COLS, 0, grid_row > 0), (tile_index + GRID_COLS, 1, grid_row < GRID_ROWS - 1), (tile_index - 1, 2, grid_col > 0), (tile_index + 1, 3, grid_col < GRID_COLS - 1))
        for neighbour, direction, present in sources:
            clipped = jnp.clip(neighbour, 0, TILES - 1).astype(jnp.int32)
            chosen = blocked[clipped][rim_blocks[clipped, direction]]
            chosen = jnp.where(present, chosen, jnp.zeros_like(chosen))
            pieces.append(chosen.reshape(HB * BLOCK, C_IN))
        pieces.append(jnp.zeros((1, C_IN), arrival.dtype))
        extended = jnp.concatenate(pieces, axis=0).astype(jnp.float32)
        lookup = jnp.where(kernel_map[tile_index] < 0, EXT_BLOCKS * BLOCK, kernel_map[tile_index]).astype(jnp.int32)
        gathered = extended[lookup]
        response = jnp.einsum('krc,kco->ro', gathered, weights_wide, precision=lax.Precision.HIGHEST)
        return response * occupied[tile_index][:, None]
    response = lax.map(one_tile, jnp.arange(TILES, dtype=jnp.int32))
    average = lax.optimization_barrier(jnp.sum(response, axis=(0, 1))) / TOTAL
    centred = (response - average) * occupied[:, :, None]
    variance = lax.optimization_barrier(jnp.sum(centred * centred, axis=(0, 1))) / TOTAL
    scaled = norm_gain * (response - average) / jnp.sqrt(variance + 1e-05) + shift_bias
    normalized = jnp.maximum(scaled, 0.0) * occupied[:, :, None]
    return normalized.reshape(TILES * TILE_ROWS, C_OUT).astype(jnp.bfloat16)
```

```python
import functools

import jax
import jax.numpy as jnp
from jax import lax
from jax.experimental import pallas as pl
from jax.experimental.pallas import tpu as pltpu
from jax.sharding import PartitionSpec as P

AXES = ("tx", "ty")
LANES = 128
BF16, F32, I32 = jnp.bfloat16, jnp.float32, jnp.int32
EMPTY = -1.0
MIB = 1 << 20


def from_behind(value, axis, steps):
    count = lax.axis_size(axis)
    leading, last = (max(0, -steps), min(count, count - steps))
    return lax.ppermute(value, axis, [(source, source + steps) for source in range(leading, last)])


def place_kernel(pair_rows, owner, voxels, out, addr_v, addr_s, wide, slots, sem):
    runs, run_len = owner.shape
    tiles = out.shape[0] // pair_rows
    earlier = lax.broadcasted_iota(I32, (run_len, run_len), 0)
    later = lax.broadcasted_iota(I32, (run_len, run_len), 1)
    upto = (earlier <= later).astype(BF16)
    tile_ids = lax.broadcasted_iota(I32, (tiles, run_len), 0)
    before = jnp.zeros((tiles, 1), F32)
    for run in range(runs):
        target = owner[run : run + 1, :]
        member = tile_ids == target
        inside = jnp.dot(member.astype(BF16), upto, preferred_element_type=F32) + before
        rank = jnp.sum(jnp.where(member, inside, 0.0), axis=0, keepdims=True)
        addr_v[run : run + 1, :] = target * pair_rows + rank.astype(I32) - 1
        before = inside[:, run_len - 1 : run_len]
    copy = pltpu.make_async_copy(addr_v, addr_s, sem)
    copy.start()
    chunk = 256

    @pl.loop(0, voxels.shape[0] // chunk)
    def _(i):
        rows = pl.ds(pl.multiple_of(i * chunk, chunk), chunk)
        wide[rows, :] = voxels[rows, :].astype(F32)

    @pl.loop(0, out.shape[0] // chunk)
    def _(i):
        rows = pl.ds(pl.multiple_of(i * chunk, chunk), chunk)
        slots[rows, :] = jnp.full((chunk, slots.shape[1]), EMPTY, F32)

    copy.wait()
    unroll = 16
    for run in range(runs):

        @pl.loop(0, run_len // unroll)
        def _(i):
            for u in range(unroll):
                place = addr_s[run, i * unroll + u]
                slots[pl.ds(place, 1), :] = wide[pl.ds(run * run_len + i * unroll + u, 1), :]

    @pl.loop(0, out.shape[0] // chunk)
    def _(i):
        rows = pl.ds(pl.multiple_of(i * chunk, chunk), chunk)
        out[rows, :] = slots[rows, :].astype(BF16)


def place(voxels, owner, tile_rows, pair_rows):
    rows, channels = voxels.shape
    runs = 8
    return pl.pallas_call(
        functools.partial(place_kernel, pair_rows),
        out_shape=jax.ShapeDtypeStruct((tile_rows, channels), BF16),
        scratch_shapes=[
            pltpu.VMEM((runs, rows // runs), I32),
            pltpu.SMEM((runs, rows // runs), I32),
            pltpu.VMEM((rows, channels), F32),
            pltpu.VMEM((tile_rows, channels), F32),
            pltpu.SemaphoreType.DMA,
        ],
        compiler_params=pltpu.CompilerParams(vmem_limit_bytes=32 * MIB),
        name="place",
    )(owner.reshape(runs, rows // runs), voxels)


def pick_kernel(block, listed, arrival, *rest):
    outs, sems = rest[:-1], rest[-1]
    count = outs[0].shape[0] // block
    copies = []
    for d, out in enumerate(outs):
        for i in range(count):
            source = pl.multiple_of(listed[d, i] * block, block)
            copies.append(
                pltpu.make_async_copy(
                    arrival.at[pl.ds(source, block), :],
                    out.at[pl.ds(i * block, block), :],
                    sems.at[d * count + i],
                )
            )
    for copy in copies:
        copy.start()
    for copy in copies:
        copy.wait()


def pick(arrival, listed, block):
    directions, count = listed.shape
    shape = jax.ShapeDtypeStruct((count * block, arrival.shape[1]), arrival.dtype)
    return pl.pallas_call(
        functools.partial(pick_kernel, block),
        in_specs=[
            pl.BlockSpec(memory_space=pltpu.SMEM),
            pl.BlockSpec(memory_space=pl.ANY),
        ],
        out_specs=[pl.BlockSpec(memory_space=pl.ANY)] * directions,
        out_shape=[shape] * directions,
        scratch_shapes=[pltpu.SemaphoreType.DMA((directions * count,))],
        name="pick_rims",
    )(listed, arrival)


def conv_kernel(block, source, kmap, arrival, rim0, rim1, rim2, rim3, weights_t, resp, occ, stats, xt, g):
    step = pl.program_id(0)
    offsets, window = kmap.shape
    channels = arrival.shape[1]
    lane = lax.broadcasted_iota(I32, (channels, LANES), 1)
    right = lane >= block
    lane_row = lax.broadcasted_iota(I32, (1, LANES), 1)
    half = jnp.where(lane_row >= block, block, 0)
    rows = lax.broadcasted_iota(I32, (LANES, LANES), 0)

    @pl.when(step == 0)
    def _():
        first = 0
        for number, part in enumerate((arrival, rim0, rim1, rim2, rim3)):
            pairs = part.shape[0] // LANES

            def turn(p, carry, part=part, first=first, number=number):
                at = pl.multiple_of(p * LANES, LANES)
                turned = part[pl.ds(at, LANES), :].astype(F32).T
                if number == 0:
                    occ[:, pl.ds(at, LANES)] = (turned[0:1, :] >= 0.0).astype(F32)
                turned = jnp.maximum(turned, 0.0)
                xt[first + 2 * p] = turned.astype(BF16)
                xt[first + 2 * p + 1] = pltpu.roll(turned, block, 1).astype(BF16)
                return carry

            lax.fori_loop(0, pairs, turn, 0, unroll=2)
            first += 2 * pairs

    blocks = window // block
    for k in range(offsets):
        for p in range(window // LANES):
            listed = kmap[k : k + 1, p * LANES : (p + 1) * LANES]
            left_block = source[k, blocks * step + 2 * p]
            right_block = source[k, blocks * step + 2 * p + 1]
            pair = jnp.where(right, xt[right_block ^ 1], xt[left_block])
            local = jnp.where(listed < 0, -1, (listed & (block - 1)) + half)
            chooser = (rows == local).astype(BF16)
            chosen = jnp.dot(pair, chooser, preferred_element_type=F32).astype(BF16)
            g[k * channels : (k + 1) * channels, p * LANES : (p + 1) * LANES] = chosen
    here = pl.ds(pl.multiple_of(step * window, window), window)
    resp[:, here] = jnp.dot(weights_t[...], g[...], preferred_element_type=F32) * occ[:, here]

    @pl.when(step == pl.num_programs(0) - 1)
    def _():
        count = resp.shape[1] // LANES

        def add(p, carry):
            total, number = carry
            at = pl.ds(pl.multiple_of(p * LANES, LANES), LANES)
            return total + resp[:, at], number + occ[:, at]

        zero = jnp.zeros((channels, LANES), F32)
        total, number = lax.fori_loop(0, count, add, (zero, jnp.zeros((1, LANES), F32)), unroll=4)
        total = jnp.sum(total, axis=1, keepdims=True)
        number = jnp.sum(number, axis=1, keepdims=True)
        mean = total / jnp.maximum(number, 1.0)

        def spread(p, squares):
            at = pl.ds(pl.multiple_of(p * LANES, LANES), LANES)
            centred = (resp[:, at] - mean) * occ[:, at]
            return squares + centred * centred

        squares = lax.fori_loop(0, count, spread, zero, unroll=4)
        squares = jnp.sum(squares, axis=1, keepdims=True)
        columns = jnp.where(lane == 0, total, jnp.where(lane == 1, squares, jnp.broadcast_to(number, (channels, LANES))))
        stats[...] = columns.T[: stats.shape[0], :]


def convolve(source, kmap, arrival, rims, weights_t, block):
    offsets, tile_rows = kmap.shape
    channels = arrival.shape[1]
    window = min(1024, tile_rows)
    ext_blocks = (tile_rows + sum(rim.shape[0] for rim in rims)) // block
    whole = pl.BlockSpec(memory_space=pltpu.VMEM)
    return pl.pallas_call(
        functools.partial(conv_kernel, block),
        grid=(tile_rows // window,),
        in_specs=[
            pl.BlockSpec(memory_space=pltpu.SMEM),
            pl.BlockSpec((offsets, window), lambda q: (0, q)),
            *[whole] * 6,
        ],
        out_specs=[whole, whole, whole],
        out_shape=[
            jax.ShapeDtypeStruct((channels, tile_rows), F32),
            jax.ShapeDtypeStruct((1, tile_rows), F32),
            jax.ShapeDtypeStruct((4, channels), F32),
        ],
        scratch_shapes=[
            pltpu.VMEM((ext_blocks, channels, LANES), BF16),
            pltpu.VMEM((offsets * channels, window), BF16),
        ],
        compiler_params=pltpu.CompilerParams(vmem_limit_bytes=56 * MIB),
        name="convolve",
    )(source, kmap, arrival, *rims, weights_t)


def finish_kernel(population, stats, gain, bias, resp, occ, out, affine):
    @pl.when(pl.program_id(0) == 0)
    def _():
        total, squares, number = stats[:, 0, :], stats[:, 1, :], stats[:, 2, :]
        average = jnp.sum(total, axis=0, keepdims=True) / population
        apart = total / jnp.maximum(number, 1.0) - average
        spread = jnp.sum(squares + number * apart * apart, axis=0, keepdims=True)
        scale = gain[...] / jnp.sqrt(spread / population + 1e-05)
        row = lax.broadcasted_iota(I32, affine.shape, 0)
        rows = jnp.where(row == 0, average, jnp.where(row == 1, scale, bias[...]))
        affine[...] = rows.T

    average, scale, shift = affine[:, 0:1], affine[:, 1:2], affine[:, 2:3]
    for p in range(resp.shape[1] // LANES):
        at = slice(p * LANES, (p + 1) * LANES)
        value = jnp.maximum((resp[:, at] - average) * scale + shift, 0.0) * occ[:, at]
        out[at, :] = value.T.astype(BF16)


def finish(stats, gain, bias, resp, occ, population):
    channels, tile_rows = resp.shape
    window = min(1024, tile_rows)
    return pl.pallas_call(
        functools.partial(finish_kernel, population),
        grid=(tile_rows // window,),
        in_specs=[
            pl.BlockSpec(memory_space=pltpu.VMEM),
            pl.BlockSpec(memory_space=pltpu.VMEM),
            pl.BlockSpec(memory_space=pltpu.VMEM),
            pl.BlockSpec((channels, window), lambda q: (0, q)),
            pl.BlockSpec((1, window), lambda q: (0, q)),
        ],
        out_specs=pl.BlockSpec((window, channels), lambda q: (q, 0)),
        out_shape=jax.ShapeDtypeStruct((tile_rows, channels), BF16),
        scratch_shapes=[pltpu.VMEM((channels, LANES), F32)],
        compiler_params=pltpu.CompilerParams(vmem_limit_bytes=32 * MIB),
        name="finish",
    )(stats, gain.reshape(1, channels), bias.reshape(1, channels), resp, occ)


def shards(voxels, owner_tile, rim_blocks, kernel_map, weights, norm_gain, shift_bias):
    devices = lax.axis_size(AXES)
    offsets, tile_rows = kernel_map.shape[1:]
    pair_rows = tile_rows // devices
    block = pair_rows
    channels = voxels.shape[1]

    def swap(value):
        return lax.all_to_all(value, AXES, split_axis=0, concat_axis=0, tiled=True)

    outgoing = place(voxels, owner_tile[:, 0], tile_rows, pair_rows)
    arrival = swap(outgoing.reshape(devices, pair_rows, channels)).reshape(tile_rows, channels)
    kmap = kernel_map[0]
    source = jnp.maximum(jnp.max(kmap.reshape(offsets, tile_rows // block, block), axis=2), 0) // block
    weights_t = weights.transpose(2, 0, 1).reshape(weights.shape[2], offsets * channels)
    picked = pick(arrival, rim_blocks[0], block)
    rims = (
        from_behind(picked[0], "tx", 1),
        from_behind(picked[1], "tx", -1),
        from_behind(picked[2], "ty", 1),
        from_behind(picked[3], "ty", -1),
    )
    resp, occ, stats = convolve(source, kmap, arrival, rims, weights_t, block)
    gathered = swap(jnp.broadcast_to(stats[None], (devices, *stats.shape)))
    return finish(gathered, norm_gain, shift_bias, resp, occ, float(voxels.shape[0] * devices))


def solution(mesh):
    return jax.shard_map(
        shards,
        mesh=mesh,
        in_specs=(
            P(AXES, None),
            P(AXES, None),
            P(AXES, None, None),
            P(AXES, None, None),
            P(),
            P(),
            P(),
        ),
        out_specs=P(AXES, None),
        check_vma=False,
    )
```

```python
import functools

import jax
import jax.numpy as jnp
from jax import lax
from jax.experimental import pallas as pl
from jax.experimental.pallas import tpu as pltpu
from jax.sharding import PartitionSpec as P

AXES = ("tx", "ty")
LANES = 128
BF16, F32, I32 = jnp.bfloat16, jnp.float32, jnp.int32
EMPTY = -1.0
MIB = 1 << 20


def from_behind(value, axis, steps):
    count = lax.axis_size(axis)
    leading, last = (max(0, -steps), min(count, count - steps))
    return lax.ppermute(value, axis, [(source, source + steps) for source in range(leading, last)])


def place_kernel(pair_rows, owner, voxels, out, addr_v, addr_s, wide, slots, sem):
    runs, run_len = owner.shape
    tiles = out.shape[0] // pair_rows
    earlier = lax.broadcasted_iota(I32, (run_len, run_len), 0)
    later = lax.broadcasted_iota(I32, (run_len, run_len), 1)
    upto = (earlier <= later).astype(BF16)
    tile_ids = lax.broadcasted_iota(I32, (tiles, run_len), 0)
    before = jnp.zeros((tiles, 1), F32)
    for run in range(runs):
        target = owner[run : run + 1, :]
        member = tile_ids == target
        inside = jnp.dot(member.astype(BF16), upto, preferred_element_type=F32) + before
        rank = jnp.sum(jnp.where(member, inside, 0.0), axis=0, keepdims=True)
        addr_v[run : run + 1, :] = target * pair_rows + rank.astype(I32) - 1
        before = inside[:, run_len - 1 : run_len]
    copy = pltpu.make_async_copy(addr_v, addr_s, sem)
    copy.start()
    chunk = 256

    @pl.loop(0, voxels.shape[0] // chunk)
    def _(i):
        rows = pl.ds(pl.multiple_of(i * chunk, chunk), chunk)
        wide[rows, :] = voxels[rows, :].astype(F32)

    @pl.loop(0, out.shape[0] // chunk)
    def _(i):
        rows = pl.ds(pl.multiple_of(i * chunk, chunk), chunk)
        slots[rows, :] = jnp.full((chunk, slots.shape[1]), EMPTY, F32)

    copy.wait()
    unroll = 16
    for run in range(runs):

        @pl.loop(0, run_len // unroll)
        def _(i):
            for u in range(unroll):
                place = addr_s[run, i * unroll + u]
                slots[pl.ds(place, 1), :] = wide[pl.ds(run * run_len + i * unroll + u, 1), :]

    @pl.loop(0, out.shape[0] // chunk)
    def _(i):
        rows = pl.ds(pl.multiple_of(i * chunk, chunk), chunk)
        out[rows, :] = slots[rows, :].astype(BF16)


def place(voxels, owner, tile_rows, pair_rows):
    rows, channels = voxels.shape
    runs = 8
    return pl.pallas_call(
        functools.partial(place_kernel, pair_rows),
        out_shape=jax.ShapeDtypeStruct((tile_rows, channels), BF16),
        scratch_shapes=[
            pltpu.VMEM((runs, rows // runs), I32),
            pltpu.SMEM((runs, rows // runs), I32),
            pltpu.VMEM((rows, channels), F32),
            pltpu.VMEM((tile_rows, channels), F32),
            pltpu.SemaphoreType.DMA,
        ],
        compiler_params=pltpu.CompilerParams(vmem_limit_bytes=32 * MIB),
        name="place",
    )(owner.reshape(runs, rows // runs), voxels)


def pick_kernel(block, listed, arrival, *outs):
    count = outs[0].shape[0] // block
    for d, out in enumerate(outs):
        for i in range(count):
            at = pl.multiple_of(listed[d, i] * block, block)
            out[i * block : (i + 1) * block, :] = arrival[pl.ds(at, block), :]


def pick(arrival, listed, block):
    directions, count = listed.shape
    shape = jax.ShapeDtypeStruct((count * block, arrival.shape[1]), arrival.dtype)
    return pl.pallas_call(
        functools.partial(pick_kernel, block),
        in_specs=[
            pl.BlockSpec(memory_space=pltpu.SMEM),
            pl.BlockSpec(memory_space=pltpu.VMEM),
        ],
        out_specs=[pl.BlockSpec(memory_space=pltpu.VMEM)] * directions,
        out_shape=[shape] * directions,
        compiler_params=pltpu.CompilerParams(vmem_limit_bytes=16 * MIB),
        name="pick_rims",
    )(listed, arrival)


def source_kernel(block, kmap, out):
    offsets, tile_rows = kmap.shape
    lane = lax.broadcasted_iota(I32, (offsets, LANES), 1)
    right = lane >= block
    found = jnp.zeros((offsets, LANES), I32)
    for p in range(tile_rows // LANES):
        listed = kmap[:, p * LANES : (p + 1) * LANES]
        for half, mine in enumerate((jnp.logical_not(right), right)):
            top = jnp.max(jnp.where(mine, listed, 0), axis=1, keepdims=True)
            found = jnp.where(lane == 2 * p + half, top, found)
    out[...] = found // block


def source_blocks(kmap, block):
    offsets, tile_rows = kmap.shape
    return pl.pallas_call(
        functools.partial(source_kernel, block),
        out_shape=jax.ShapeDtypeStruct((offsets, tile_rows // block), I32),
        compiler_params=pltpu.CompilerParams(vmem_limit_bytes=16 * MIB),
        name="source_blocks",
    )(kmap)


def conv_kernel(block, source, kmap, arrival, rim0, rim1, rim2, rim3, weights_t, resp, occ, stats, xt, g):
    step = pl.program_id(0)
    offsets, window = kmap.shape
    channels = arrival.shape[1]
    lane = lax.broadcasted_iota(I32, (channels, LANES), 1)
    right = lane >= block
    lane_row = lax.broadcasted_iota(I32, (1, LANES), 1)
    half = jnp.where(lane_row >= block, block, 0)
    rows = lax.broadcasted_iota(I32, (LANES, LANES), 0)

    @pl.when(step == 0)
    def _():
        same = (rows == lane).astype(BF16)
        first = 0
        for number, part in enumerate((arrival, rim0, rim1, rim2, rim3)):
            pairs = part.shape[0] // LANES

            def turn(p, carry, part=part, first=first, number=number):
                at = pl.multiple_of(p * LANES, LANES)
                straight = part[pl.ds(at, LANES), :]
                swapped = jnp.concatenate((straight[block:], straight[:block]), axis=0)
                both = jnp.concatenate((straight, swapped), axis=0)
                turned = lax.dot_general(same, both, (((1,), (1,)), ((), ())), preferred_element_type=F32)
                if number == 0:
                    occ[:, pl.ds(at, LANES)] = (turned[0:1, :LANES] >= 0.0).astype(F32)
                turned = jnp.maximum(turned, 0.0).astype(BF16)
                xt[first + 2 * p] = turned[:, :LANES]
                xt[first + 2 * p + 1] = turned[:, LANES:]
                return carry

            lax.fori_loop(0, pairs, turn, 0, unroll=4)
            first += 2 * pairs

    blocks = window // block
    for k in range(offsets):
        for p in range(window // LANES):
            listed = kmap[k : k + 1, p * LANES : (p + 1) * LANES]
            left_block = source[k, blocks * step + 2 * p]
            right_block = source[k, blocks * step + 2 * p + 1]
            pair = jnp.where(right, xt[right_block ^ 1], xt[left_block])
            local = jnp.where(listed < 0, -1, (listed & (block - 1)) + half)
            chooser = (rows == local).astype(BF16)
            chosen = jnp.dot(pair, chooser, preferred_element_type=F32).astype(BF16)
            g[k * channels : (k + 1) * channels, p * LANES : (p + 1) * LANES] = chosen
    here = pl.ds(pl.multiple_of(step * window, window), window)
    resp[:, here] = jnp.dot(weights_t[...], g[...], preferred_element_type=F32) * occ[:, here]

    @pl.when(step == pl.num_programs(0) - 1)
    def _():
        count = resp.shape[1] // LANES

        def add(p, carry):
            total, number = carry
            at = pl.ds(pl.multiple_of(p * LANES, LANES), LANES)
            return total + resp[:, at], number + occ[:, at]

        zero = jnp.zeros((channels, LANES), F32)
        total, number = lax.fori_loop(0, count, add, (zero, jnp.zeros((1, LANES), F32)), unroll=4)
        total = jnp.sum(total, axis=1, keepdims=True)
        number = jnp.sum(number, axis=1, keepdims=True)
        mean = total / jnp.maximum(number, 1.0)

        def spread(p, squares):
            at = pl.ds(pl.multiple_of(p * LANES, LANES), LANES)
            centred = (resp[:, at] - mean) * occ[:, at]
            return squares + centred * centred

        squares = lax.fori_loop(0, count, spread, zero, unroll=4)
        squares = jnp.sum(squares, axis=1, keepdims=True)
        columns = jnp.where(lane == 0, total, jnp.where(lane == 1, squares, jnp.broadcast_to(number, (channels, LANES))))
        stats[...] = columns.T[: stats.shape[0], :]


def convolve(source, kmap, arrival, rims, weights_t, block):
    offsets, tile_rows = kmap.shape
    channels = arrival.shape[1]
    window = min(1024, tile_rows)
    ext_blocks = (tile_rows + sum(rim.shape[0] for rim in rims)) // block
    whole = pl.BlockSpec(memory_space=pltpu.VMEM)
    return pl.pallas_call(
        functools.partial(conv_kernel, block),
        grid=(tile_rows // window,),
        in_specs=[
            pl.BlockSpec(memory_space=pltpu.SMEM),
            pl.BlockSpec((offsets, window), lambda q: (0, q)),
            *[whole] * 6,
        ],
        out_specs=[whole, whole, whole],
        out_shape=[
            jax.ShapeDtypeStruct((channels, tile_rows), F32),
            jax.ShapeDtypeStruct((1, tile_rows), F32),
            jax.ShapeDtypeStruct((4, channels), F32),
        ],
        scratch_shapes=[
            pltpu.VMEM((ext_blocks, channels, LANES), BF16),
            pltpu.VMEM((offsets * channels, window), BF16),
        ],
        compiler_params=pltpu.CompilerParams(vmem_limit_bytes=56 * MIB),
        name="convolve",
    )(source, kmap, arrival, *rims, weights_t)


def finish_kernel(population, stats, gain, bias, resp, occ, out, affine):
    @pl.when(pl.program_id(0) == 0)
    def _():
        total, squares, number = stats[:, 0, :], stats[:, 1, :], stats[:, 2, :]
        average = jnp.sum(total, axis=0, keepdims=True) / population
        apart = total / jnp.maximum(number, 1.0) - average
        spread = jnp.sum(squares + number * apart * apart, axis=0, keepdims=True)
        scale = gain[...] / jnp.sqrt(spread / population + 1e-05)
        row = lax.broadcasted_iota(I32, affine.shape, 0)
        rows = jnp.where(row == 0, average, jnp.where(row == 1, scale, bias[...]))
        affine[...] = rows.T

    average, scale, shift = affine[:, 0:1], affine[:, 1:2], affine[:, 2:3]
    for p in range(resp.shape[1] // LANES):
        at = slice(p * LANES, (p + 1) * LANES)
        value = jnp.maximum((resp[:, at] - average) * scale + shift, 0.0) * occ[:, at]
        out[at, :] = value.T.astype(BF16)


def finish(stats, gain, bias, resp, occ, population):
    channels, tile_rows = resp.shape
    window = min(1024, tile_rows)
    return pl.pallas_call(
        functools.partial(finish_kernel, population),
        grid=(tile_rows // window,),
        in_specs=[
            pl.BlockSpec(memory_space=pltpu.VMEM),
            pl.BlockSpec(memory_space=pltpu.VMEM),
            pl.BlockSpec(memory_space=pltpu.VMEM),
            pl.BlockSpec((channels, window), lambda q: (0, q)),
            pl.BlockSpec((1, window), lambda q: (0, q)),
        ],
        out_specs=pl.BlockSpec((window, channels), lambda q: (q, 0)),
        out_shape=jax.ShapeDtypeStruct((tile_rows, channels), BF16),
        scratch_shapes=[pltpu.VMEM((channels, LANES), F32)],
        compiler_params=pltpu.CompilerParams(vmem_limit_bytes=32 * MIB),
        name="finish",
    )(stats, gain.reshape(1, channels), bias.reshape(1, channels), resp, occ)


def shards(voxels, owner_tile, rim_blocks, kernel_map, weights, norm_gain, shift_bias):
    devices = lax.axis_size(AXES)
    offsets, tile_rows = kernel_map.shape[1:]
    pair_rows = tile_rows // devices
    block = pair_rows
    channels = voxels.shape[1]

    def swap(value):
        return lax.all_to_all(value, AXES, split_axis=0, concat_axis=0, tiled=True)

    outgoing = place(voxels, owner_tile[:, 0], tile_rows, pair_rows)
    arrival = swap(outgoing.reshape(devices, pair_rows, channels)).reshape(tile_rows, channels)
    kmap = kernel_map[0]
    source = source_blocks(kmap, block)
    weights_t = weights.transpose(2, 0, 1).reshape(weights.shape[2], offsets * channels)
    picked = pick(arrival, rim_blocks[0], block)
    rims = (
        from_behind(picked[0], "tx", 1),
        from_behind(picked[1], "tx", -1),
        from_behind(picked[2], "ty", 1),
        from_behind(picked[3], "ty", -1),
    )
    resp, occ, stats = convolve(source, kmap, arrival, rims, weights_t, block)
    gathered = swap(jnp.broadcast_to(stats[None], (devices, *stats.shape)))
    return finish(gathered, norm_gain, shift_bias, resp, occ, float(voxels.shape[0] * devices))


def solution(mesh):
    return jax.shard_map(
        shards,
        mesh=mesh,
        in_specs=(
            P(AXES, None),
            P(AXES, None),
            P(AXES, None, None),
            P(AXES, None, None),
            P(),
            P(),
            P(),
        ),
        out_specs=P(AXES, None),
        check_vma=False,
    )
```

```python
import functools

import jax
import jax.numpy as jnp
from jax import lax
from jax.experimental import pallas as pl
from jax.experimental.pallas import tpu as pltpu
from jax.sharding import PartitionSpec as P

AXES = ("tx", "ty")
LANES = 128
BF16, F32, I32 = jnp.bfloat16, jnp.float32, jnp.int32
EMPTY = -1.0
MIB = 1 << 20


def from_behind(value, axis, steps):
    count = lax.axis_size(axis)
    leading, last = (max(0, -steps), min(count, count - steps))
    return lax.ppermute(value, axis, [(source, source + steps) for source in range(leading, last)])


def place_kernel(pair_rows, owner, voxels, out, addr_v, addr_s, wide, slots, sem):
    runs, run_len = owner.shape
    tiles = out.shape[0] // pair_rows
    earlier = lax.broadcasted_iota(I32, (run_len, run_len), 0)
    later = lax.broadcasted_iota(I32, (run_len, run_len), 1)
    upto = (earlier <= later).astype(BF16)
    tile_ids = lax.broadcasted_iota(I32, (tiles, run_len), 0)
    before = jnp.zeros((tiles, 1), F32)
    for run in range(runs):
        target = owner[run : run + 1, :]
        member = tile_ids == target
        inside = jnp.dot(member.astype(BF16), upto, preferred_element_type=F32) + before
        rank = jnp.sum(jnp.where(member, inside, 0.0), axis=0, keepdims=True)
        addr_v[run : run + 1, :] = target * pair_rows + rank.astype(I32) - 1
        before = inside[:, run_len - 1 : run_len]
    copy = pltpu.make_async_copy(addr_v, addr_s, sem)
    copy.start()
    chunk = 256

    @pl.loop(0, voxels.shape[0] // chunk)
    def _(i):
        rows = pl.ds(pl.multiple_of(i * chunk, chunk), chunk)
        wide[rows, :] = voxels[rows, :].astype(F32)

    @pl.loop(0, out.shape[0] // chunk)
    def _(i):
        rows = pl.ds(pl.multiple_of(i * chunk, chunk), chunk)
        slots[rows, :] = jnp.full((chunk, slots.shape[1]), EMPTY, F32)

    copy.wait()
    unroll = 16
    for run in range(runs):

        @pl.loop(0, run_len // unroll)
        def _(i):
            for u in range(unroll):
                place = addr_s[run, i * unroll + u]
                slots[pl.ds(place, 1), :] = wide[pl.ds(run * run_len + i * unroll + u, 1), :]

    @pl.loop(0, out.shape[0] // chunk)
    def _(i):
        rows = pl.ds(pl.multiple_of(i * chunk, chunk), chunk)
        out[rows, :] = slots[rows, :].astype(BF16)


def place(voxels, owner, tile_rows, pair_rows):
    rows, channels = voxels.shape
    runs = 8
    return pl.pallas_call(
        functools.partial(place_kernel, pair_rows),
        out_shape=jax.ShapeDtypeStruct((tile_rows, channels), BF16),
        scratch_shapes=[
            pltpu.VMEM((runs, rows // runs), I32),
            pltpu.SMEM((runs, rows // runs), I32),
            pltpu.VMEM((rows, channels), F32),
            pltpu.VMEM((tile_rows, channels), F32),
            pltpu.SemaphoreType.DMA,
        ],
        compiler_params=pltpu.CompilerParams(vmem_limit_bytes=32 * MIB),
        name="place",
    )(owner.reshape(runs, rows // runs), voxels)


def pick_kernel(block, listed, arrival, *outs):
    count = outs[0].shape[0] // block
    for d, out in enumerate(outs):
        for i in range(count):
            at = pl.multiple_of(listed[d, i] * block, block)
            out[i * block : (i + 1) * block, :] = arrival[pl.ds(at, block), :]


def pick(arrival, listed, block):
    directions, count = listed.shape
    shape = jax.ShapeDtypeStruct((count * block, arrival.shape[1]), arrival.dtype)
    return pl.pallas_call(
        functools.partial(pick_kernel, block),
        in_specs=[
            pl.BlockSpec(memory_space=pltpu.SMEM),
            pl.BlockSpec(memory_space=pltpu.VMEM),
        ],
        out_specs=[pl.BlockSpec(memory_space=pltpu.VMEM)] * directions,
        out_shape=[shape] * directions,
        compiler_params=pltpu.CompilerParams(vmem_limit_bytes=16 * MIB),
        name="pick_rims",
    )(listed, arrival)


def source_kernel(block, kmap, out):
    offsets, tile_rows = kmap.shape[0], kmap.shape[2]
    lane = lax.broadcasted_iota(I32, (offsets, LANES), 1)
    right = lane >= block
    found = jnp.zeros((offsets, LANES), I32)
    for p in range(tile_rows // LANES):
        listed = kmap[:, 0, p * LANES : (p + 1) * LANES]
        for half, mine in enumerate((jnp.logical_not(right), right)):
            top = jnp.max(jnp.where(mine, listed, 0), axis=1, keepdims=True)
            found = jnp.where(lane == 2 * p + half, top, found)
    out[...] = found // block


def source_blocks(kmap, block):
    offsets, _, tile_rows = kmap.shape
    return pl.pallas_call(
        functools.partial(source_kernel, block),
        out_shape=jax.ShapeDtypeStruct((offsets, tile_rows // block), I32),
        compiler_params=pltpu.CompilerParams(vmem_limit_bytes=16 * MIB),
        name="source_blocks",
    )(kmap)


def same_of(channels):
    row = lax.broadcasted_iota(I32, (channels, channels), 0)
    lane = lax.broadcasted_iota(I32, (channels, channels), 1)
    return (row == lane).astype(BF16)


def turned(same, rows):
    return lax.dot_general(same, rows, (((1,), (1,)), ((), ())), preferred_element_type=F32)


def turn_pair(same, part, p, block):
    straight = part[pl.ds(pl.multiple_of(p * LANES, LANES), LANES), :]
    swapped = jnp.concatenate((straight[block:], straight[:block]), axis=0)
    return turned(same, jnp.concatenate((straight, swapped), axis=0))


def turn_kernel(block, arrival, weights, xt, occ, weights_t):
    channels = arrival.shape[1]
    same = same_of(channels)

    def turn(p, carry):
        both = turn_pair(same, arrival, p, block)
        occ[:, pl.ds(pl.multiple_of(p * LANES, LANES), LANES)] = (both[0:1, :LANES] >= 0.0).astype(F32)
        both = jnp.maximum(both, 0.0).astype(BF16)
        xt[2 * p] = both[:, :LANES]
        xt[2 * p + 1] = both[:, LANES:]
        return carry

    lax.fori_loop(0, arrival.shape[0] // LANES, turn, 0, unroll=8)
    for k in range(weights.shape[0]):
        weights_t[:, k * channels : (k + 1) * channels] = turned(same, weights[k]).astype(BF16)


def turn_local(arrival, weights, block):
    tile_rows, channels = arrival.shape
    offsets = weights.shape[0]
    return pl.pallas_call(
        functools.partial(turn_kernel, block),
        out_shape=[
            jax.ShapeDtypeStruct((tile_rows // block, channels, LANES), BF16),
            jax.ShapeDtypeStruct((1, tile_rows), F32),
            jax.ShapeDtypeStruct((weights.shape[2], offsets * channels), BF16),
        ],
        compiler_params=pltpu.CompilerParams(vmem_limit_bytes=16 * MIB),
        name="turn_local",
    )(arrival, weights)


def conv_kernel(block, window, source, kmap, xt_local, rim0, rim1, rim2, rim3, weights_t, occ, resp, stats, xt, g):
    offsets, tile_rows = kmap.shape[0], kmap.shape[2]
    channels = xt_local.shape[1]
    same = same_of(channels)
    lane = lax.broadcasted_iota(I32, (channels, LANES), 1)
    right = lane >= block
    half = jnp.where(lax.broadcasted_iota(I32, (1, LANES), 1) >= block, block, 0)
    rows16 = lax.broadcasted_iota(I32, (LANES, LANES), 0).astype(jnp.int16)
    none = jnp.zeros((LANES, LANES), BF16)

    def keep(i, carry):
        xt[i] = xt_local[i]
        return carry

    first = xt_local.shape[0]
    lax.fori_loop(0, first, keep, 0, unroll=8)
    for part in (rim0, rim1, rim2, rim3):
        pairs = part.shape[0] // LANES

        def turn(p, carry, part=part, first=first):
            both = jnp.maximum(turn_pair(same, part, p, block), 0.0).astype(BF16)
            xt[first + 2 * p] = both[:, :LANES]
            xt[first + 2 * p + 1] = both[:, LANES:]
            return carry

        lax.fori_loop(0, pairs, turn, 0, unroll=8)
        first += 2 * pairs

    blocks = window // block

    def convolve_window(step, total):
        def pair_of(k, p):
            left_block = source[k, blocks * step + 2 * p]
            right_block = source[k, blocks * step + 2 * p + 1]
            return jnp.where(right, xt[right_block ^ 1], xt[left_block])

        def chooser_of(k, p):
            at = pl.ds(pl.multiple_of(step * window, window) + p * LANES, LANES)
            listed = kmap[k, :, at]
            local = jnp.where(listed < 0, -1, (listed & (block - 1)) + half)
            local = jnp.broadcast_to(local, (LANES, LANES)).astype(jnp.int16)
            return jnp.where(rows16 == local, jnp.ones((), BF16), jnp.zeros((), BF16))

        for k in range(offsets):
            for p in range(0, window // LANES, 2):
                to = slice(k * channels, (k + 1) * channels)
                if k == offsets // 2:
                    for q in (p, p + 1):
                        g[to, q * LANES : (q + 1) * LANES] = xt[blocks * step + 2 * q]
                    continue
                pairs = jnp.concatenate((pair_of(k, p), pair_of(k, p + 1)), axis=1)
                chooser = jnp.concatenate(
                    (
                        jnp.concatenate((chooser_of(k, p), none), axis=1),
                        jnp.concatenate((none, chooser_of(k, p + 1)), axis=1),
                    ),
                    axis=0,
                )
                chosen = jnp.dot(pairs, chooser, preferred_element_type=F32).astype(BF16)
                g[to, p * LANES : (p + 2) * LANES] = chosen
        here = pl.ds(pl.multiple_of(step * window, window), window)
        value = jnp.dot(weights_t[...], g[...], preferred_element_type=F32) * occ[:, here]
        resp[:, here] = value
        for p in range(window // LANES):
            total = total + value[:, p * LANES : (p + 1) * LANES]
        return total

    zero = jnp.zeros((channels, LANES), F32)
    total = lax.fori_loop(0, tile_rows // window, convolve_window, zero)
    total = jnp.sum(total, axis=1, keepdims=True)
    number = jnp.sum(occ[...], axis=1, keepdims=True)
    mean = total / jnp.maximum(number, 1.0)

    def spread(p, squares):
        at = pl.ds(pl.multiple_of(p * LANES, LANES), LANES)
        centred = (resp[:, at] - mean) * occ[:, at]
        return squares + centred * centred

    squares = lax.fori_loop(0, tile_rows // LANES, spread, zero, unroll=4)
    squares = jnp.sum(squares, axis=1, keepdims=True)
    columns = jnp.where(lane == 0, total, jnp.where(lane == 1, squares, jnp.broadcast_to(number, (channels, LANES))))
    stats[...] = columns.T[: stats.shape[0], :]


def convolve(source, kmap, xt_local, rims, weights_t, occ, block):
    offsets, _, tile_rows = kmap.shape
    local_blocks, channels, _ = xt_local.shape
    window = min(1024, tile_rows)
    ext_blocks = local_blocks + sum(rim.shape[0] for rim in rims) // block
    whole = pl.BlockSpec(memory_space=pltpu.VMEM)
    return pl.pallas_call(
        functools.partial(conv_kernel, block, window),
        in_specs=[pl.BlockSpec(memory_space=pltpu.SMEM), *[whole] * 8],
        out_specs=[whole, whole],
        out_shape=[
            jax.ShapeDtypeStruct((channels, tile_rows), F32),
            jax.ShapeDtypeStruct((4, channels), F32),
        ],
        scratch_shapes=[
            pltpu.VMEM((ext_blocks, channels, LANES), BF16),
            pltpu.VMEM((offsets * channels, window), BF16),
        ],
        compiler_params=pltpu.CompilerParams(vmem_limit_bytes=40 * MIB),
        name="convolve",
    )(source, kmap, xt_local, *rims, weights_t, occ)


def finish_kernel(population, stats, gain, bias, resp, occ, out, affine):
    @pl.when(pl.program_id(0) == 0)
    def _():
        total, squares, number = stats[:, 0, :], stats[:, 1, :], stats[:, 2, :]
        average = jnp.sum(total, axis=0, keepdims=True) / population
        apart = total / jnp.maximum(number, 1.0) - average
        spread = jnp.sum(squares + number * apart * apart, axis=0, keepdims=True)
        scale = gain[...] / jnp.sqrt(spread / population + 1e-05)
        row = lax.broadcasted_iota(I32, affine.shape, 0)
        rows = jnp.where(row == 0, average, jnp.where(row == 1, scale, bias[...]))
        affine[...] = rows.T

    average, scale, shift = affine[:, 0:1], affine[:, 1:2], affine[:, 2:3]
    for p in range(resp.shape[1] // LANES):
        at = slice(p * LANES, (p + 1) * LANES)
        value = jnp.maximum((resp[:, at] - average) * scale + shift, 0.0) * occ[:, at]
        out[at, :] = value.T.astype(BF16)


def finish(stats, gain, bias, resp, occ, population):
    channels, tile_rows = resp.shape
    window = min(1024, tile_rows)
    return pl.pallas_call(
        functools.partial(finish_kernel, population),
        grid=(tile_rows // window,),
        in_specs=[
            pl.BlockSpec(memory_space=pltpu.VMEM),
            pl.BlockSpec(memory_space=pltpu.VMEM),
            pl.BlockSpec(memory_space=pltpu.VMEM),
            pl.BlockSpec((channels, window), lambda q: (0, q)),
            pl.BlockSpec((1, window), lambda q: (0, q)),
        ],
        out_specs=pl.BlockSpec((window, channels), lambda q: (q, 0)),
        out_shape=jax.ShapeDtypeStruct((tile_rows, channels), BF16),
        scratch_shapes=[pltpu.VMEM((channels, LANES), F32)],
        compiler_params=pltpu.CompilerParams(vmem_limit_bytes=32 * MIB),
        name="finish",
    )(stats, gain.reshape(1, channels), bias.reshape(1, channels), resp, occ)


def shards(voxels, owner_tile, rim_blocks, kernel_map, weights, norm_gain, shift_bias):
    devices = lax.axis_size(AXES)
    offsets, tile_rows = kernel_map.shape[1:]
    pair_rows = tile_rows // devices
    block = pair_rows
    channels = voxels.shape[1]

    def swap(value):
        return lax.all_to_all(value, AXES, split_axis=0, concat_axis=0, tiled=True)

    outgoing = place(voxels, owner_tile, tile_rows, pair_rows)
    arrival = swap(outgoing.reshape(devices, pair_rows, channels)).reshape(tile_rows, channels)
    kmap = kernel_map.transpose(1, 0, 2)
    source = source_blocks(kmap, block)
    picked = pick(arrival, rim_blocks[0], block)
    rims = (
        from_behind(picked[0], "tx", 1),
        from_behind(picked[1], "tx", -1),
        from_behind(picked[2], "ty", 1),
        from_behind(picked[3], "ty", -1),
    )
    xt, occ, weights_t = turn_local(arrival, weights, block)
    resp, stats = convolve(source, kmap, xt, rims, weights_t, occ, block)
    gathered = swap(jnp.broadcast_to(stats[None], (devices, *stats.shape)))
    return finish(gathered, norm_gain, shift_bias, resp, occ, float(voxels.shape[0] * devices))


def solution(mesh):
    return jax.shard_map(
        shards,
        mesh=mesh,
        in_specs=(
            P(AXES, None),
            P(AXES, None),
            P(AXES, None, None),
            P(AXES, None, None),
            P(),
            P(),
            P(),
        ),
        out_specs=P(AXES, None),
        check_vma=False,
    )
```

```python
import functools

import jax
import jax.numpy as jnp
from jax import lax
from jax.experimental import pallas as pl
from jax.experimental.pallas import tpu as pltpu
from jax.sharding import PartitionSpec as P

AXES = ("tx", "ty")
LANES = 128
BF16, F32, I32 = jnp.bfloat16, jnp.float32, jnp.int32
EMPTY = -1.0
MIB = 1 << 20


def from_behind(value, axis, steps):
    count = lax.axis_size(axis)
    leading, last = (max(0, -steps), min(count, count - steps))
    return lax.ppermute(value, axis, [(source, source + steps) for source in range(leading, last)])


def place_kernel(pair_rows, owner, voxels, out, held, addr_v, addr_s, wide, slots, sems):
    rows = voxels.shape[0]
    tiles = out.shape[0] // pair_rows
    fetch = pltpu.make_async_copy(voxels, held, sems.at[0])
    fetch.start()
    run_len = min(512, rows)
    earlier = lax.broadcasted_iota(I32, (run_len, run_len), 0)
    later = lax.broadcasted_iota(I32, (run_len, run_len), 1)
    upto = (earlier <= later).astype(BF16)
    tile_ids = lax.broadcasted_iota(I32, (tiles, run_len), 0)
    before = jnp.zeros((tiles, 1), F32)
    for first in range(0, rows, run_len):
        target = owner[:, first : first + run_len]
        member = tile_ids == target
        inside = jnp.dot(member.astype(BF16), upto, preferred_element_type=F32) + before
        rank = jnp.sum(jnp.where(member, inside, 0.0), axis=0, keepdims=True)
        address = target * pair_rows + rank.astype(I32) - 1
        for j in range(0, run_len, LANES):
            line = (first + j) // LANES
            addr_v[line : line + 1, :] = address[:, j : j + LANES]
        before = inside[:, run_len - 1 : run_len]
    copy = pltpu.make_async_copy(addr_v, addr_s, sems.at[1])
    copy.start()
    chunk = 256

    @pl.loop(0, out.shape[0] // chunk)
    def _(i):
        here = pl.ds(pl.multiple_of(i * chunk, chunk), chunk)
        slots[here, :] = jnp.full((chunk, slots.shape[1]), EMPTY, F32)

    fetch.wait()

    @pl.loop(0, rows // chunk)
    def _(i):
        here = pl.ds(pl.multiple_of(i * chunk, chunk), chunk)
        wide[here, :] = held[here, :].astype(F32)

    copy.wait()

    @pl.loop(0, rows // LANES)
    def _(line):
        for u in range(LANES):
            slots[pl.ds(addr_s[line, u], 1), :] = wide[pl.ds(line * LANES + u, 1), :]

    @pl.loop(0, out.shape[0] // chunk)
    def _(i):
        here = pl.ds(pl.multiple_of(i * chunk, chunk), chunk)
        out[here, :] = slots[here, :].astype(BF16)


def place(voxels, owner_tile, tile_rows, pair_rows):
    rows, channels = voxels.shape
    return pl.pallas_call(
        functools.partial(place_kernel, pair_rows),
        in_specs=[pl.BlockSpec(memory_space=pltpu.VMEM), pl.BlockSpec(memory_space=pl.ANY)],
        out_specs=pl.BlockSpec(memory_space=pltpu.VMEM),
        out_shape=jax.ShapeDtypeStruct((tile_rows, channels), BF16),
        scratch_shapes=[
            pltpu.VMEM((rows, channels), BF16),
            pltpu.VMEM((rows // LANES, LANES), I32),
            pltpu.SMEM((rows // LANES, LANES), I32),
            pltpu.VMEM((rows, channels), F32),
            pltpu.VMEM((tile_rows, channels), F32),
            pltpu.SemaphoreType.DMA((2,)),
        ],
        compiler_params=pltpu.CompilerParams(vmem_limit_bytes=32 * MIB),
        name="place",
    )(owner_tile.T, voxels)


def pick_kernel(block, listed, arrival, *outs):
    count = outs[0].shape[0] // block
    for d, out in enumerate(outs):
        for i in range(count):
            at = pl.multiple_of(listed[d, i] * block, block)
            out[i * block : (i + 1) * block, :] = arrival[pl.ds(at, block), :]


def pick(arrival, listed, block):
    directions, count = listed.shape
    shape = jax.ShapeDtypeStruct((count * block, arrival.shape[1]), arrival.dtype)
    return pl.pallas_call(
        functools.partial(pick_kernel, block),
        in_specs=[
            pl.BlockSpec(memory_space=pltpu.SMEM),
            pl.BlockSpec(memory_space=pltpu.VMEM),
        ],
        out_specs=[pl.BlockSpec(memory_space=pltpu.VMEM)] * directions,
        out_shape=[shape] * directions,
        compiler_params=pltpu.CompilerParams(vmem_limit_bytes=16 * MIB),
        name="pick_rims",
    )(listed, arrival)


def source_kernel(block, kmap, out):
    offsets, tile_rows = kmap.shape[0], kmap.shape[2]
    lane = lax.broadcasted_iota(I32, (offsets, LANES), 1)
    right = lane >= block
    found = jnp.zeros((offsets, LANES), I32)
    for p in range(tile_rows // LANES):
        listed = kmap[:, 0, p * LANES : (p + 1) * LANES]
        for half, mine in enumerate((jnp.logical_not(right), right)):
            top = jnp.max(jnp.where(mine, listed, 0), axis=1, keepdims=True)
            found = jnp.where(lane == 2 * p + half, top, found)
    out[...] = found // block


def source_blocks(kmap, block):
    offsets, _, tile_rows = kmap.shape
    return pl.pallas_call(
        functools.partial(source_kernel, block),
        out_shape=jax.ShapeDtypeStruct((offsets, tile_rows // block), I32),
        compiler_params=pltpu.CompilerParams(vmem_limit_bytes=16 * MIB),
        name="source_blocks",
    )(kmap)


def same_of(channels):
    row = lax.broadcasted_iota(I32, (channels, channels), 0)
    lane = lax.broadcasted_iota(I32, (channels, channels), 1)
    return (row == lane).astype(BF16)


def turned(same, rows):
    return lax.dot_general(same, rows, (((1,), (1,)), ((), ())), preferred_element_type=F32)


def turn_pair(same, part, p, block):
    straight = part[pl.ds(pl.multiple_of(p * LANES, LANES), LANES), :]
    swapped = jnp.concatenate((straight[block:], straight[:block]), axis=0)
    return turned(same, jnp.concatenate((straight, swapped), axis=0))


def turn_kernel(block, arrival, weights, xt, occ, weights_t):
    channels = arrival.shape[1]
    same = same_of(channels)

    def turn(p, carry):
        both = turn_pair(same, arrival, p, block)
        occ[:, pl.ds(pl.multiple_of(p * LANES, LANES), LANES)] = (both[0:1, :LANES] >= 0.0).astype(F32)
        both = jnp.maximum(both, 0.0).astype(BF16)
        xt[2 * p] = both[:, :LANES]
        xt[2 * p + 1] = both[:, LANES:]
        return carry

    lax.fori_loop(0, arrival.shape[0] // LANES, turn, 0, unroll=8)
    for k in range(weights.shape[0]):
        weights_t[:, k * channels : (k + 1) * channels] = turned(same, weights[k]).astype(BF16)


def turn_local(arrival, weights, block):
    tile_rows, channels = arrival.shape
    offsets = weights.shape[0]
    return pl.pallas_call(
        functools.partial(turn_kernel, block),
        out_shape=[
            jax.ShapeDtypeStruct((tile_rows // block, channels, LANES), BF16),
            jax.ShapeDtypeStruct((1, tile_rows), F32),
            jax.ShapeDtypeStruct((weights.shape[2], offsets * channels), BF16),
        ],
        compiler_params=pltpu.CompilerParams(vmem_limit_bytes=16 * MIB),
        name="turn_local",
    )(arrival, weights)


def conv_kernel(block, window, source, kmap, xt_local, rim0, rim1, rim2, rim3, weights_t, occ, resp, stats, xt, g):
    offsets, tile_rows = kmap.shape[0], kmap.shape[2]
    channels = xt_local.shape[1]
    same = same_of(channels)
    lane = lax.broadcasted_iota(I32, (channels, LANES), 1)
    right = lane >= block
    half = jnp.where(lax.broadcasted_iota(I32, (1, LANES), 1) >= block, block, 0)
    rows16 = lax.broadcasted_iota(I32, (LANES, LANES), 0).astype(jnp.int16)
    none = jnp.zeros((LANES, LANES), BF16)

    def keep(i, carry):
        xt[i] = xt_local[i]
        return carry

    first = xt_local.shape[0]
    lax.fori_loop(0, first, keep, 0, unroll=8)
    for part in (rim0, rim1, rim2, rim3):
        pairs = part.shape[0] // LANES

        def turn(p, carry, part=part, first=first):
            both = jnp.maximum(turn_pair(same, part, p, block), 0.0).astype(BF16)
            xt[first + 2 * p] = both[:, :LANES]
            xt[first + 2 * p + 1] = both[:, LANES:]
            return carry

        lax.fori_loop(0, pairs, turn, 0, unroll=8)
        first += 2 * pairs

    blocks = window // block

    def convolve_window(step, total):
        def pair_of(k, p):
            left_block = source[k, blocks * step + 2 * p]
            right_block = source[k, blocks * step + 2 * p + 1]
            return jnp.where(right, xt[right_block ^ 1], xt[left_block])

        def chooser_of(k, p):
            at = pl.ds(pl.multiple_of(step * window, window) + p * LANES, LANES)
            listed = kmap[k, :, at]
            local = jnp.where(listed < 0, -1, (listed & (block - 1)) + half)
            local = jnp.broadcast_to(local, (LANES, LANES)).astype(jnp.int16)
            return jnp.where(rows16 == local, jnp.ones((), BF16), jnp.zeros((), BF16))

        for k in range(offsets):
            for p in range(0, window // LANES, 2):
                to = slice(k * channels, (k + 1) * channels)
                if k == offsets // 2:
                    for q in (p, p + 1):
                        g[to, q * LANES : (q + 1) * LANES] = xt[blocks * step + 2 * q]
                    continue
                pairs = jnp.concatenate((pair_of(k, p), pair_of(k, p + 1)), axis=1)
                chooser = jnp.concatenate(
                    (
                        jnp.concatenate((chooser_of(k, p), none), axis=1),
                        jnp.concatenate((none, chooser_of(k, p + 1)), axis=1),
                    ),
                    axis=0,
                )
                chosen = jnp.dot(pairs, chooser, preferred_element_type=F32).astype(BF16)
                g[to, p * LANES : (p + 2) * LANES] = chosen
        here = pl.ds(pl.multiple_of(step * window, window), window)
        value = jnp.dot(weights_t[...], g[...], preferred_element_type=F32) * occ[:, here]
        resp[:, here] = value
        for p in range(window // LANES):
            total = total + value[:, p * LANES : (p + 1) * LANES]
        return total

    zero = jnp.zeros((channels, LANES), F32)
    total = lax.fori_loop(0, tile_rows // window, convolve_window, zero)
    total = jnp.sum(total, axis=1, keepdims=True)
    number = jnp.sum(occ[...], axis=1, keepdims=True)
    mean = total / jnp.maximum(number, 1.0)

    def spread(p, squares):
        at = pl.ds(pl.multiple_of(p * LANES, LANES), LANES)
        centred = (resp[:, at] - mean) * occ[:, at]
        return squares + centred * centred

    squares = lax.fori_loop(0, tile_rows // LANES, spread, zero, unroll=4)
    squares = jnp.sum(squares, axis=1, keepdims=True)
    columns = jnp.where(lane == 0, total, jnp.where(lane == 1, squares, jnp.broadcast_to(number, (channels, LANES))))
    lines = columns.T
    line = jnp.concatenate((lines[0:1], lines[1:2], lines[2:3]), axis=1)

    def tell(i, carry):
        stats[i] = line
        return carry

    lax.fori_loop(0, stats.shape[0], tell, 0, unroll=8)


def convolve(source, kmap, xt_local, rims, weights_t, occ, block):
    offsets, _, tile_rows = kmap.shape
    local_blocks, channels, _ = xt_local.shape
    window = min(1024, tile_rows)
    ext_blocks = local_blocks + sum(rim.shape[0] for rim in rims) // block
    whole = pl.BlockSpec(memory_space=pltpu.VMEM)
    return pl.pallas_call(
        functools.partial(conv_kernel, block, window),
        in_specs=[pl.BlockSpec(memory_space=pltpu.SMEM), *[whole] * 8],
        out_specs=[whole, whole],
        out_shape=[
            jax.ShapeDtypeStruct((channels, tile_rows), F32),
            jax.ShapeDtypeStruct((tile_rows // block, 1, 3 * channels), F32),
        ],
        scratch_shapes=[
            pltpu.VMEM((ext_blocks, channels, LANES), BF16),
            pltpu.VMEM((offsets * channels, window), BF16),
        ],
        compiler_params=pltpu.CompilerParams(vmem_limit_bytes=40 * MIB),
        name="convolve",
    )(source, kmap, xt_local, *rims, weights_t, occ)


def finish_kernel(population, stats, gain, bias, resp, occ, out, stage, sems):
    channels, tile_rows = resp.shape
    total = stats[:, 0, :channels]
    squares = stats[:, 0, channels : 2 * channels]
    number = stats[:, 0, 2 * channels :]
    average = jnp.sum(total, axis=0, keepdims=True) / population
    apart = total / jnp.maximum(number, 1.0) - average
    spread = jnp.sum(squares + number * apart * apart, axis=0, keepdims=True)
    scale = gain[...] / jnp.sqrt(spread / population + 1e-05)
    row = lax.broadcasted_iota(I32, (LANES, channels), 0)
    affine = jnp.where(row == 0, average, jnp.where(row == 1, scale, bias[...])).T
    average, scale, shift = affine[:, 0:1], affine[:, 1:2], affine[:, 2:3]
    count = sems.shape[0]
    part = tile_rows // count
    copies = []
    for c in range(count):

        def turn(p, carry, c=c):
            at = pl.ds(pl.multiple_of(c * part + p * LANES, LANES), LANES)
            value = jnp.maximum((resp[:, at] - average) * scale + shift, 0.0) * occ[:, at]
            stage[at, :] = value.T.astype(BF16)
            return carry

        lax.fori_loop(0, part // LANES, turn, 0, unroll=8)
        here = slice(c * part, (c + 1) * part)
        copies.append(pltpu.make_async_copy(stage.at[here, :], out.at[here, :], sems.at[c]))
        copies[-1].start()
    for copy in copies:
        copy.wait()


def finish(stats, gain, bias, resp, occ, population):
    channels, tile_rows = resp.shape
    whole = pl.BlockSpec(memory_space=pltpu.VMEM)
    return pl.pallas_call(
        functools.partial(finish_kernel, population),
        in_specs=[whole] * 5,
        out_specs=pl.BlockSpec(memory_space=pl.ANY),
        out_shape=jax.ShapeDtypeStruct((tile_rows, channels), BF16),
        scratch_shapes=[pltpu.VMEM((tile_rows, channels), BF16), pltpu.SemaphoreType.DMA((8,))],
        compiler_params=pltpu.CompilerParams(vmem_limit_bytes=16 * MIB),
        name="finish",
    )(stats, gain.reshape(1, channels), bias.reshape(1, channels), resp, occ)


def shards(voxels, owner_tile, rim_blocks, kernel_map, weights, norm_gain, shift_bias):
    devices = lax.axis_size(AXES)
    offsets, tile_rows = kernel_map.shape[1:]
    pair_rows = tile_rows // devices
    block = pair_rows
    channels = voxels.shape[1]

    def swap(value):
        return lax.all_to_all(value, AXES, split_axis=0, concat_axis=0, tiled=True)

    outgoing = place(voxels, owner_tile, tile_rows, pair_rows)
    arrival = swap(outgoing.reshape(devices, pair_rows, channels)).reshape(tile_rows, channels)
    kmap = kernel_map.transpose(1, 0, 2)
    source = source_blocks(kmap, block)
    picked = pick(arrival, rim_blocks[0], block)
    rims = (
        from_behind(picked[0], "tx", 1),
        from_behind(picked[1], "tx", -1),
        from_behind(picked[2], "ty", 1),
        from_behind(picked[3], "ty", -1),
    )
    xt, occ, weights_t = turn_local(arrival, weights, block)
    resp, stats = convolve(source, kmap, xt, rims, weights_t, occ, block)
    gathered = swap(stats)
    return finish(gathered, norm_gain, shift_bias, resp, occ, float(voxels.shape[0] * devices))


def solution(mesh):
    return jax.shard_map(
        shards,
        mesh=mesh,
        in_specs=(
            P(AXES, None),
            P(AXES, None),
            P(AXES, None, None),
            P(AXES, None, None),
            P(),
            P(),
            P(),
        ),
        out_specs=P(AXES, None),
        check_vma=False,
    )
```

```python
import functools

import jax
import jax.numpy as jnp
from jax import lax
from jax.experimental import pallas as pl
from jax.experimental.pallas import tpu as pltpu
from jax.sharding import PartitionSpec as P

AXES = ("tx", "ty")
LANES = 128
BF16, F32, I32 = jnp.bfloat16, jnp.float32, jnp.int32
EMPTY = -1.0
MIB = 1 << 20


def exchanged(value, axis, first):
    pairs = range(first, lax.axis_size(axis) - 1, 2)
    return lax.ppermute(value, axis, [way for i in pairs for way in ((i, i + 1), (i + 1, i))])


def place_kernel(pair_rows, owner, voxels, out, held, addr_v, addr_s, wide, slots, sems):
    rows = voxels.shape[0]
    tiles = out.shape[0] // pair_rows
    fetch = pltpu.make_async_copy(voxels, held, sems.at[0])
    fetch.start()
    run_len = min(512, rows)
    earlier = lax.broadcasted_iota(I32, (run_len, run_len), 0)
    later = lax.broadcasted_iota(I32, (run_len, run_len), 1)
    upto = (earlier <= later).astype(BF16)
    tile_ids = lax.broadcasted_iota(I32, (tiles, run_len), 0)
    before = jnp.zeros((tiles, 1), F32)
    for first in range(0, rows, run_len):
        target = owner[:, first : first + run_len]
        member = tile_ids == target
        inside = jnp.dot(member.astype(BF16), upto, preferred_element_type=F32) + before
        rank = jnp.sum(jnp.where(member, inside, 0.0), axis=0, keepdims=True)
        address = target * pair_rows + rank.astype(I32) - 1
        for j in range(0, run_len, LANES):
            line = (first + j) // LANES
            addr_v[line : line + 1, :] = address[:, j : j + LANES]
        before = inside[:, run_len - 1 : run_len]
    copy = pltpu.make_async_copy(addr_v, addr_s, sems.at[1])
    copy.start()
    chunk = 256

    @pl.loop(0, out.shape[0] // chunk)
    def _(i):
        here = pl.ds(pl.multiple_of(i * chunk, chunk), chunk)
        slots[here, :] = jnp.full((chunk, slots.shape[1]), EMPTY, F32)

    fetch.wait()

    @pl.loop(0, rows // chunk)
    def _(i):
        here = pl.ds(pl.multiple_of(i * chunk, chunk), chunk)
        wide[here, :] = held[here, :].astype(F32)

    copy.wait()

    @pl.loop(0, rows // LANES)
    def _(line):
        for u in range(LANES):
            slots[pl.ds(addr_s[line, u], 1), :] = wide[pl.ds(line * LANES + u, 1), :]

    @pl.loop(0, out.shape[0] // chunk)
    def _(i):
        here = pl.ds(pl.multiple_of(i * chunk, chunk), chunk)
        out[here, :] = slots[here, :].astype(BF16)


def place(voxels, owner_tile, tile_rows, pair_rows):
    rows, channels = voxels.shape
    return pl.pallas_call(
        functools.partial(place_kernel, pair_rows),
        in_specs=[pl.BlockSpec(memory_space=pltpu.VMEM), pl.BlockSpec(memory_space=pl.ANY)],
        out_specs=pl.BlockSpec(memory_space=pltpu.VMEM),
        out_shape=jax.ShapeDtypeStruct((tile_rows, channels), BF16),
        scratch_shapes=[
            pltpu.VMEM((rows, channels), BF16),
            pltpu.VMEM((rows // LANES, LANES), I32),
            pltpu.SMEM((rows // LANES, LANES), I32),
            pltpu.VMEM((rows, channels), F32),
            pltpu.VMEM((tile_rows, channels), F32),
            pltpu.SemaphoreType.DMA((2,)),
        ],
        compiler_params=pltpu.CompilerParams(vmem_limit_bytes=32 * MIB),
        name="place",
    )(owner_tile.T, voxels)


def pick_kernel(block, listed, ways, arrival, *outs):
    count = outs[0].shape[0] // block
    for d, out in enumerate(outs):
        for i in range(count):
            at = pl.multiple_of(listed[ways[d], i] * block, block)
            out[i * block : (i + 1) * block, :] = arrival[pl.ds(at, block), :]


def pick(arrival, listed, ways, block):
    directions, count = listed.shape
    shape = jax.ShapeDtypeStruct((count * block, arrival.shape[1]), arrival.dtype)
    return pl.pallas_call(
        functools.partial(pick_kernel, block),
        in_specs=[
            pl.BlockSpec(memory_space=pltpu.SMEM),
            pl.BlockSpec(memory_space=pltpu.SMEM),
            pl.BlockSpec(memory_space=pltpu.VMEM),
        ],
        out_specs=[pl.BlockSpec(memory_space=pltpu.VMEM)] * directions,
        out_shape=[shape] * directions,
        compiler_params=pltpu.CompilerParams(vmem_limit_bytes=16 * MIB),
        name="pick_rims",
    )(listed, ways, arrival)


def source_kernel(block, kmap, out):
    offsets, tile_rows = kmap.shape[0], kmap.shape[2]
    lane = lax.broadcasted_iota(I32, (offsets, LANES), 1)
    right = lane >= block
    found = jnp.zeros((offsets, LANES), I32)
    for p in range(tile_rows // LANES):
        listed = kmap[:, 0, p * LANES : (p + 1) * LANES]
        for half, mine in enumerate((jnp.logical_not(right), right)):
            top = jnp.max(jnp.where(mine, listed, 0), axis=1, keepdims=True)
            found = jnp.where(lane == 2 * p + half, top, found)
    out[...] = found // block


def source_blocks(kmap, block):
    offsets, _, tile_rows = kmap.shape
    return pl.pallas_call(
        functools.partial(source_kernel, block),
        out_shape=jax.ShapeDtypeStruct((offsets, tile_rows // block), I32),
        compiler_params=pltpu.CompilerParams(vmem_limit_bytes=16 * MIB),
        name="source_blocks",
    )(kmap)


def same_of(channels):
    row = lax.broadcasted_iota(I32, (channels, channels), 0)
    lane = lax.broadcasted_iota(I32, (channels, channels), 1)
    return (row == lane).astype(BF16)


def turned(same, rows):
    return lax.dot_general(same, rows, (((1,), (1,)), ((), ())), preferred_element_type=F32)


def turn_pair(same, part, p, block):
    straight = part[pl.ds(pl.multiple_of(p * LANES, LANES), LANES), :]
    swapped = jnp.concatenate((straight[block:], straight[:block]), axis=0)
    return turned(same, jnp.concatenate((straight, swapped), axis=0))


def turn_kernel(block, arrival, weights, xt, occ, weights_t):
    channels = arrival.shape[1]
    same = same_of(channels)

    def turn(p, carry):
        both = turn_pair(same, arrival, p, block)
        occ[:, pl.ds(pl.multiple_of(p * LANES, LANES), LANES)] = (both[0:1, :LANES] >= 0.0).astype(F32)
        both = jnp.maximum(both, 0.0).astype(BF16)
        xt[2 * p] = both[:, :LANES]
        xt[2 * p + 1] = both[:, LANES:]
        return carry

    lax.fori_loop(0, arrival.shape[0] // LANES, turn, 0, unroll=8)
    for k in range(weights.shape[0]):
        weights_t[:, k * channels : (k + 1) * channels] = turned(same, weights[k]).astype(BF16)


def turn_local(arrival, weights, block):
    tile_rows, channels = arrival.shape
    offsets = weights.shape[0]
    return pl.pallas_call(
        functools.partial(turn_kernel, block),
        out_shape=[
            jax.ShapeDtypeStruct((tile_rows // block, channels, LANES), BF16),
            jax.ShapeDtypeStruct((1, tile_rows), F32),
            jax.ShapeDtypeStruct((weights.shape[2], offsets * channels), BF16),
        ],
        compiler_params=pltpu.CompilerParams(vmem_limit_bytes=16 * MIB),
        name="turn_local",
    )(arrival, weights)


def conv_kernel(block, window, source, ways, kmap, xt_local, rim0, rim1, rim2, rim3, weights_t, occ, resp, stats, xt, g):
    offsets, tile_rows = kmap.shape[0], kmap.shape[2]
    channels = xt_local.shape[1]
    same = same_of(channels)
    lane = lax.broadcasted_iota(I32, (channels, LANES), 1)
    right = lane >= block
    half = jnp.where(lax.broadcasted_iota(I32, (1, LANES), 1) >= block, block, 0)
    rows16 = lax.broadcasted_iota(I32, (LANES, LANES), 0).astype(jnp.int16)
    none = jnp.zeros((LANES, LANES), BF16)

    def keep(i, carry):
        xt[i] = xt_local[i]
        return carry

    local_blocks = xt_local.shape[0]
    lax.fori_loop(0, local_blocks, keep, 0, unroll=8)
    for d, part in enumerate((rim0, rim1, rim2, rim3)):
        first = local_blocks + (ways[d] ^ 1) * (part.shape[0] // block)

        def turn(p, carry, part=part, first=first):
            both = jnp.maximum(turn_pair(same, part, p, block), 0.0).astype(BF16)
            xt[first + 2 * p] = both[:, :LANES]
            xt[first + 2 * p + 1] = both[:, LANES:]
            return carry

        lax.fori_loop(0, part.shape[0] // LANES, turn, 0, unroll=8)

    blocks = window // block

    def convolve_window(step, total):
        def pair_of(k, p):
            left_block = source[k, blocks * step + 2 * p]
            right_block = source[k, blocks * step + 2 * p + 1]
            return jnp.where(right, xt[right_block ^ 1], xt[left_block])

        def chooser_of(k, p):
            at = pl.ds(pl.multiple_of(step * window, window) + p * LANES, LANES)
            listed = kmap[k, :, at]
            local = jnp.where(listed < 0, -1, (listed & (block - 1)) + half)
            local = jnp.broadcast_to(local, (LANES, LANES)).astype(jnp.int16)
            return jnp.where(rows16 == local, jnp.ones((), BF16), jnp.zeros((), BF16))

        for k in range(offsets):
            for p in range(0, window // LANES, 2):
                to = slice(k * channels, (k + 1) * channels)
                if k == offsets // 2:
                    for q in (p, p + 1):
                        g[to, q * LANES : (q + 1) * LANES] = xt[blocks * step + 2 * q]
                    continue
                pairs = jnp.concatenate((pair_of(k, p), pair_of(k, p + 1)), axis=1)
                chooser = jnp.concatenate(
                    (
                        jnp.concatenate((chooser_of(k, p), none), axis=1),
                        jnp.concatenate((none, chooser_of(k, p + 1)), axis=1),
                    ),
                    axis=0,
                )
                chosen = jnp.dot(pairs, chooser, preferred_element_type=F32).astype(BF16)
                g[to, p * LANES : (p + 2) * LANES] = chosen
        here = pl.ds(pl.multiple_of(step * window, window), window)
        value = jnp.dot(weights_t[...], g[...], preferred_element_type=F32) * occ[:, here]
        resp[:, here] = value
        for p in range(window // LANES):
            total = total + value[:, p * LANES : (p + 1) * LANES]
        return total

    zero = jnp.zeros((channels, LANES), F32)
    total = lax.fori_loop(0, tile_rows // window, convolve_window, zero)
    total = jnp.sum(total, axis=1, keepdims=True)
    number = jnp.sum(occ[...], axis=1, keepdims=True)
    mean = total / jnp.maximum(number, 1.0)

    def spread(p, squares):
        at = pl.ds(pl.multiple_of(p * LANES, LANES), LANES)
        centred = (resp[:, at] - mean) * occ[:, at]
        return squares + centred * centred

    squares = lax.fori_loop(0, tile_rows // LANES, spread, zero, unroll=4)
    squares = jnp.sum(squares, axis=1, keepdims=True)
    columns = jnp.where(lane == 0, total, jnp.where(lane == 1, squares, jnp.broadcast_to(number, (channels, LANES))))
    lines = columns.T
    line = jnp.concatenate((lines[0:1], lines[1:2], lines[2:3]), axis=1)

    def tell(i, carry):
        stats[i] = line
        return carry

    lax.fori_loop(0, stats.shape[0], tell, 0, unroll=8)


def convolve(source, ways, kmap, xt_local, rims, weights_t, occ, block):
    offsets, _, tile_rows = kmap.shape
    local_blocks, channels, _ = xt_local.shape
    window = min(1024, tile_rows)
    ext_blocks = local_blocks + sum(rim.shape[0] for rim in rims) // block
    whole = pl.BlockSpec(memory_space=pltpu.VMEM)
    return pl.pallas_call(
        functools.partial(conv_kernel, block, window),
        in_specs=[pl.BlockSpec(memory_space=pltpu.SMEM)] * 2 + [whole] * 8,
        out_specs=[whole, whole],
        out_shape=[
            jax.ShapeDtypeStruct((channels, tile_rows), F32),
            jax.ShapeDtypeStruct((tile_rows // block, 1, 3 * channels), F32),
        ],
        scratch_shapes=[
            pltpu.VMEM((ext_blocks, channels, LANES), BF16),
            pltpu.VMEM((offsets * channels, window), BF16),
        ],
        compiler_params=pltpu.CompilerParams(vmem_limit_bytes=40 * MIB),
        name="convolve",
    )(source, ways, kmap, xt_local, *rims, weights_t, occ)


def finish_kernel(population, stats, gain, bias, resp, occ, out, stage, sems):
    channels, tile_rows = resp.shape
    total = stats[:, 0, :channels]
    squares = stats[:, 0, channels : 2 * channels]
    number = stats[:, 0, 2 * channels :]
    average = jnp.sum(total, axis=0, keepdims=True) / population
    apart = total / jnp.maximum(number, 1.0) - average
    spread = jnp.sum(squares + number * apart * apart, axis=0, keepdims=True)
    scale = gain[...] / jnp.sqrt(spread / population + 1e-05)
    row = lax.broadcasted_iota(I32, (LANES, channels), 0)
    affine = jnp.where(row == 0, average, jnp.where(row == 1, scale, bias[...])).T
    average, scale, shift = affine[:, 0:1], affine[:, 1:2], affine[:, 2:3]
    count = sems.shape[0]
    part = tile_rows // count
    copies = []
    for c in range(count):

        def turn(p, carry, c=c):
            at = pl.ds(pl.multiple_of(c * part + p * LANES, LANES), LANES)
            value = jnp.maximum((resp[:, at] - average) * scale + shift, 0.0) * occ[:, at]
            stage[at, :] = value.T.astype(BF16)
            return carry

        lax.fori_loop(0, part // LANES, turn, 0, unroll=8)
        here = slice(c * part, (c + 1) * part)
        copies.append(pltpu.make_async_copy(stage.at[here, :], out.at[here, :], sems.at[c]))
        copies[-1].start()
    for copy in copies:
        copy.wait()


def finish(stats, gain, bias, resp, occ, population):
    channels, tile_rows = resp.shape
    whole = pl.BlockSpec(memory_space=pltpu.VMEM)
    return pl.pallas_call(
        functools.partial(finish_kernel, population),
        in_specs=[whole] * 5,
        out_specs=pl.BlockSpec(memory_space=pl.ANY),
        out_shape=jax.ShapeDtypeStruct((tile_rows, channels), BF16),
        scratch_shapes=[pltpu.VMEM((tile_rows, channels), BF16), pltpu.SemaphoreType.DMA((8,))],
        compiler_params=pltpu.CompilerParams(vmem_limit_bytes=16 * MIB),
        name="finish",
    )(stats, gain.reshape(1, channels), bias.reshape(1, channels), resp, occ)


def shards(voxels, owner_tile, rim_blocks, kernel_map, weights, norm_gain, shift_bias):
    devices = lax.axis_size(AXES)
    offsets, tile_rows = kernel_map.shape[1:]
    pair_rows = tile_rows // devices
    block = pair_rows
    channels = voxels.shape[1]

    def swap(value):
        return lax.all_to_all(value, AXES, split_axis=0, concat_axis=0, tiled=True)

    outgoing = place(voxels, owner_tile, tile_rows, pair_rows)
    arrival = swap(outgoing.reshape(devices, pair_rows, channels)).reshape(tile_rows, channels)
    kmap = kernel_map.transpose(1, 0, 2)
    source = source_blocks(kmap, block)
    odd_row, odd_col = lax.axis_index("tx") % 2, lax.axis_index("ty") % 2
    ways = jnp.stack((odd_row, 1 - odd_row, 2 + odd_col, 3 - odd_col)).astype(I32)
    picked = pick(arrival, rim_blocks[0], ways, block)
    rims = (
        exchanged(picked[0], "tx", 0),
        exchanged(picked[1], "tx", 1),
        exchanged(picked[2], "ty", 0),
        exchanged(picked[3], "ty", 1),
    )
    xt, occ, weights_t = turn_local(arrival, weights, block)
    resp, stats = convolve(source, ways, kmap, xt, rims, weights_t, occ, block)
    gathered = swap(stats)
    return finish(gathered, norm_gain, shift_bias, resp, occ, float(voxels.shape[0] * devices))


def solution(mesh):
    return jax.shard_map(
        shards,
        mesh=mesh,
        in_specs=(
            P(AXES, None),
            P(AXES, None),
            P(AXES, None, None),
            P(AXES, None, None),
            P(),
            P(),
            P(),
        ),
        out_specs=P(AXES, None),
        check_vma=False,
    )
```

```python
import functools

import jax
import jax.numpy as jnp
from jax import lax
from jax.experimental import pallas as pl
from jax.experimental.pallas import tpu as pltpu
from jax.sharding import PartitionSpec as P

AXES = ("tx", "ty")
LANES = 128
BF16, F32, I32, I16 = jnp.bfloat16, jnp.float32, jnp.int32, jnp.int16
EMPTY = -1.0
MIB = 1 << 20
LANE_TURN = 4


def exchanged(value, axis, first):
    pairs = range(first, lax.axis_size(axis) - 1, 2)
    return lax.ppermute(value, axis, [way for i in pairs for way in ((i, i + 1), (i + 1, i))])


def place_kernel(pair_rows, owner, voxels, out, held, addr_v, addr_s, wide, slots, sems):
    rows = voxels.shape[0]
    tiles = out.shape[0] // pair_rows
    fetch = pltpu.make_async_copy(voxels, held, sems.at[0])
    fetch.start()
    run_len = min(512, rows)
    earlier = lax.broadcasted_iota(I32, (run_len, run_len), 0)
    later = lax.broadcasted_iota(I32, (run_len, run_len), 1)
    upto = (earlier <= later).astype(BF16)
    tile_ids = lax.broadcasted_iota(I32, (tiles, run_len), 0)
    before = jnp.zeros((tiles, 1), F32)
    for first in range(0, rows, run_len):
        target = owner[:, first : first + run_len]
        member = tile_ids == target
        inside = jnp.dot(member.astype(BF16), upto, preferred_element_type=F32) + before
        rank = jnp.sum(jnp.where(member, inside, 0.0), axis=0, keepdims=True)
        address = target * pair_rows + rank.astype(I32) - 1
        for j in range(0, run_len, LANES):
            line = (first + j) // LANES
            addr_v[line : line + 1, :] = address[:, j : j + LANES]
        before = inside[:, run_len - 1 : run_len]
    copy = pltpu.make_async_copy(addr_v, addr_s, sems.at[1])
    copy.start()
    chunk = 256

    @pl.loop(0, out.shape[0] // chunk)
    def _(i):
        here = pl.ds(pl.multiple_of(i * chunk, chunk), chunk)
        slots[here, :] = jnp.full((chunk, slots.shape[1]), EMPTY, F32)

    fetch.wait()

    @pl.loop(0, rows // chunk)
    def _(i):
        here = pl.ds(pl.multiple_of(i * chunk, chunk), chunk)
        wide[here, :] = held[here, :].astype(F32)

    copy.wait()

    @pl.loop(0, rows // LANES)
    def _(line):
        for u in range(LANES):
            slots[pl.ds(addr_s[line, u], 1), :] = wide[pl.ds(line * LANES + u, 1), :]

    @pl.loop(0, out.shape[0] // chunk)
    def _(i):
        here = pl.ds(pl.multiple_of(i * chunk, chunk), chunk)
        out[here, :] = slots[here, :].astype(BF16)


def place(voxels, owner_tile, tile_rows, pair_rows):
    rows, channels = voxels.shape
    return pl.pallas_call(
        functools.partial(place_kernel, pair_rows),
        in_specs=[pl.BlockSpec(memory_space=pltpu.VMEM), pl.BlockSpec(memory_space=pl.ANY)],
        out_specs=pl.BlockSpec(memory_space=pltpu.VMEM),
        out_shape=jax.ShapeDtypeStruct((tile_rows, channels), BF16),
        scratch_shapes=[
            pltpu.VMEM((rows, channels), BF16),
            pltpu.VMEM((rows // LANES, LANES), I32),
            pltpu.SMEM((rows // LANES, LANES), I32),
            pltpu.VMEM((rows, channels), F32),
            pltpu.VMEM((tile_rows, channels), F32),
            pltpu.SemaphoreType.DMA((2,)),
        ],
        compiler_params=pltpu.CompilerParams(vmem_limit_bytes=32 * MIB),
        name="place",
    )(owner_tile.T, voxels)


def pick_kernel(block, listed, ways, arrival, *outs):
    count = outs[0].shape[0] // block
    for d, out in enumerate(outs):
        for i in range(count):
            at = pl.multiple_of(listed[ways[d], i] * block, block)
            out[i * block : (i + 1) * block, :] = arrival[pl.ds(at, block), :]


def pick(arrival, listed, ways, block):
    directions, count = listed.shape
    shape = jax.ShapeDtypeStruct((count * block, arrival.shape[1]), arrival.dtype)
    return pl.pallas_call(
        functools.partial(pick_kernel, block),
        in_specs=[
            pl.BlockSpec(memory_space=pltpu.SMEM),
            pl.BlockSpec(memory_space=pltpu.SMEM),
            pl.BlockSpec(memory_space=pltpu.VMEM),
        ],
        out_specs=[pl.BlockSpec(memory_space=pltpu.VMEM)] * directions,
        out_shape=[shape] * directions,
        compiler_params=pltpu.CompilerParams(vmem_limit_bytes=16 * MIB),
        name="pick_rims",
    )(listed, ways, arrival)


def source_kernel(block, kmap, out):
    offsets, tile_rows = kmap.shape[0], kmap.shape[2]
    lane = lax.broadcasted_iota(I32, (offsets, LANES), 1)
    right = lane >= block
    found = jnp.zeros((offsets, LANES), I32)
    for p in range(tile_rows // LANES):
        listed = kmap[:, 0, p * LANES : (p + 1) * LANES]
        for half, mine in enumerate((jnp.logical_not(right), right)):
            top = jnp.max(jnp.where(mine, listed, 0), axis=1, keepdims=True)
            found = jnp.where(lane == 2 * p + half, top, found)
    out[...] = found // block


def source_blocks(kmap, block):
    offsets, _, tile_rows = kmap.shape
    return pl.pallas_call(
        functools.partial(source_kernel, block),
        out_shape=jax.ShapeDtypeStruct((offsets, tile_rows // block), I32),
        compiler_params=pltpu.CompilerParams(vmem_limit_bytes=16 * MIB),
        name="source_blocks",
    )(kmap)


def lane_gather(value, index):
    numbers = lax.GatherDimensionNumbers(
        offset_dims=(),
        collapsed_slice_dims=(1,),
        start_index_map=(1,),
        operand_batching_dims=(0,),
        start_indices_batching_dims=(0,),
    )
    mode = lax.GatherScatterMode.PROMISE_IN_BOUNDS
    return lax.gather(value, index[..., None], numbers, (1, 1), mode=mode)


def same_of(channels):
    row = lax.broadcasted_iota(I32, (channels, channels), 0)
    lane = lax.broadcasted_iota(I32, (channels, channels), 1)
    return (row == lane).astype(BF16)


def turned(same, rows):
    return lax.dot_general(same, rows, (((1,), (1,)), ((), ())), preferred_element_type=F32)


def turn_pair(same, part, p, block):
    straight = part[pl.ds(pl.multiple_of(p * LANES, LANES), LANES), :]
    swapped = jnp.concatenate((straight[block:], straight[:block]), axis=0)
    return turned(same, jnp.concatenate((straight, swapped), axis=0))


def turn_kernel(block, arrival, weights, xt, occ, weights_t):
    channels = arrival.shape[1]
    same = same_of(channels)

    def turn(p, carry):
        both = turn_pair(same, arrival, p, block)
        occ[:, pl.ds(pl.multiple_of(p * LANES, LANES), LANES)] = (both[0:1, :LANES] >= 0.0).astype(F32)
        both = jnp.maximum(both, 0.0).astype(BF16)
        xt[2 * p] = both[:, :LANES]
        xt[2 * p + 1] = both[:, LANES:]
        return carry

    lax.fori_loop(0, arrival.shape[0] // LANES, turn, 0, unroll=8)
    for k in range(weights.shape[0]):
        weights_t[:, k * channels : (k + 1) * channels] = turned(same, weights[k]).astype(BF16)


def turn_local(arrival, weights, block):
    tile_rows, channels = arrival.shape
    offsets = weights.shape[0]
    return pl.pallas_call(
        functools.partial(turn_kernel, block),
        out_shape=[
            jax.ShapeDtypeStruct((tile_rows // block, channels, LANES), BF16),
            jax.ShapeDtypeStruct((1, tile_rows), F32),
            jax.ShapeDtypeStruct((weights.shape[2], offsets * channels), BF16),
        ],
        compiler_params=pltpu.CompilerParams(vmem_limit_bytes=16 * MIB),
        name="turn_local",
    )(arrival, weights)


def conv_kernel(block, window, source, ways, kmap, xt_local, rim0, rim1, rim2, rim3, weights_t, occ, resp, stats, xt, g):
    offsets, tile_rows = kmap.shape[0], kmap.shape[2]
    channels = xt_local.shape[1]
    same = same_of(channels)
    lane = lax.broadcasted_iota(I32, (channels, LANES), 1)
    right = lane >= block
    half = jnp.where(lax.broadcasted_iota(I32, (1, LANES), 1) >= block, block, 0)
    rows16 = lax.broadcasted_iota(I32, (LANES, LANES), 0).astype(I16)
    none = jnp.zeros((LANES, LANES), BF16)

    def keep(i, carry):
        xt[i] = xt_local[i]
        return carry

    local_blocks = xt_local.shape[0]
    lax.fori_loop(0, local_blocks, keep, 0, unroll=8)
    for d, part in enumerate((rim0, rim1, rim2, rim3)):
        first = local_blocks + (ways[d] ^ 1) * (part.shape[0] // block)

        def turn(p, carry, part=part, first=first):
            both = jnp.maximum(turn_pair(same, part, p, block), 0.0).astype(BF16)
            xt[first + 2 * p] = both[:, :LANES]
            xt[first + 2 * p + 1] = both[:, LANES:]
            return carry

        lax.fori_loop(0, part.shape[0] // LANES, turn, 0, unroll=8)

    blocks = window // block

    def convolve_window(step, total):
        def pair_of(k, p):
            left_block = source[k, blocks * step + 2 * p]
            right_block = source[k, blocks * step + 2 * p + 1]
            return jnp.where(right, xt[right_block ^ 1], xt[left_block])

        def chooser_of(k, p):
            at = pl.ds(pl.multiple_of(step * window, window) + p * LANES, LANES)
            listed = kmap[k, :, at]
            local = jnp.where(listed < 0, -1, (listed & (block - 1)) + half)
            local = jnp.broadcast_to(local, (LANES, LANES)).astype(I16)
            return jnp.where(rows16 == local, jnp.ones((), BF16), jnp.zeros((), BF16))

        for k in range(offsets):
            for p in range(0, window // LANES, 2):
                to = slice(k * channels, (k + 1) * channels)
                if k == offsets // 2:
                    for q in (p, p + 1):
                        g[to, q * LANES : (q + 1) * LANES] = xt[blocks * step + 2 * q]
                    continue
                if k % LANE_TURN == 0:
                    for q in (p, p + 1):
                        at = pl.ds(pl.multiple_of(step * window, window) + q * LANES, LANES)
                        listed = kmap[k, :, at]
                        index = jnp.broadcast_to((listed & (block - 1)) + half, (channels, LANES)).astype(I16)
                        there = jnp.broadcast_to(listed, (channels, LANES)).astype(I16) >= 0
                        chosen = jnp.where(there, lane_gather(pair_of(k, q), index), jnp.zeros((), BF16))
                        g[to, q * LANES : (q + 1) * LANES] = chosen
                    continue
                pairs = jnp.concatenate((pair_of(k, p), pair_of(k, p + 1)), axis=1)
                chooser = jnp.concatenate(
                    (
                        jnp.concatenate((chooser_of(k, p), none), axis=1),
                        jnp.concatenate((none, chooser_of(k, p + 1)), axis=1),
                    ),
                    axis=0,
                )
                chosen = jnp.dot(pairs, chooser, preferred_element_type=F32).astype(BF16)
                g[to, p * LANES : (p + 2) * LANES] = chosen
        here = pl.ds(pl.multiple_of(step * window, window), window)
        value = jnp.dot(weights_t[...], g[...], preferred_element_type=F32) * occ[:, here]
        resp[:, here] = value
        for p in range(window // LANES):
            total = total + value[:, p * LANES : (p + 1) * LANES]
        return total

    zero = jnp.zeros((channels, LANES), F32)
    total = lax.fori_loop(0, tile_rows // window, convolve_window, zero)
    total = jnp.sum(total, axis=1, keepdims=True)
    number = jnp.sum(occ[...], axis=1, keepdims=True)
    mean = total / jnp.maximum(number, 1.0)

    def spread(p, squares):
        at = pl.ds(pl.multiple_of(p * LANES, LANES), LANES)
        centred = (resp[:, at] - mean) * occ[:, at]
        return squares + centred * centred

    squares = lax.fori_loop(0, tile_rows // LANES, spread, zero, unroll=4)
    squares = jnp.sum(squares, axis=1, keepdims=True)
    columns = jnp.where(lane == 0, total, jnp.where(lane == 1, squares, jnp.broadcast_to(number, (channels, LANES))))
    lines = columns.T
    line = jnp.concatenate((lines[0:1], lines[1:2], lines[2:3]), axis=1)

    def tell(i, carry):
        stats[i] = line
        return carry

    lax.fori_loop(0, stats.shape[0], tell, 0, unroll=8)


def convolve(source, ways, kmap, xt_local, rims, weights_t, occ, block):
    offsets, _, tile_rows = kmap.shape
    local_blocks, channels, _ = xt_local.shape
    window = min(1024, tile_rows)
    ext_blocks = local_blocks + sum(rim.shape[0] for rim in rims) // block
    whole = pl.BlockSpec(memory_space=pltpu.VMEM)
    return pl.pallas_call(
        functools.partial(conv_kernel, block, window),
        in_specs=[pl.BlockSpec(memory_space=pltpu.SMEM)] * 2 + [whole] * 8,
        out_specs=[whole, whole],
        out_shape=[
            jax.ShapeDtypeStruct((channels, tile_rows), F32),
            jax.ShapeDtypeStruct((tile_rows // block, 1, 3 * channels), F32),
        ],
        scratch_shapes=[
            pltpu.VMEM((ext_blocks, channels, LANES), BF16),
            pltpu.VMEM((offsets * channels, window), BF16),
        ],
        compiler_params=pltpu.CompilerParams(vmem_limit_bytes=40 * MIB),
        name="convolve",
    )(source, ways, kmap, xt_local, *rims, weights_t, occ)


def finish_kernel(population, stats, gain, bias, resp, occ, out, stage, sems):
    channels, tile_rows = resp.shape
    total = stats[:, 0, :channels]
    squares = stats[:, 0, channels : 2 * channels]
    number = stats[:, 0, 2 * channels :]
    average = jnp.sum(total, axis=0, keepdims=True) / population
    apart = total / jnp.maximum(number, 1.0) - average
    spread = jnp.sum(squares + number * apart * apart, axis=0, keepdims=True)
    scale = gain[...] / jnp.sqrt(spread / population + 1e-05)
    row = lax.broadcasted_iota(I32, (LANES, channels), 0)
    affine = jnp.where(row == 0, average, jnp.where(row == 1, scale, bias[...])).T
    average, scale, shift = affine[:, 0:1], affine[:, 1:2], affine[:, 2:3]
    count = sems.shape[0]
    part = tile_rows // count
    copies = []
    for c in range(count):

        def turn(p, carry, c=c):
            at = pl.ds(pl.multiple_of(c * part + p * LANES, LANES), LANES)
            value = jnp.maximum((resp[:, at] - average) * scale + shift, 0.0) * occ[:, at]
            stage[at, :] = value.T.astype(BF16)
            return carry

        lax.fori_loop(0, part // LANES, turn, 0, unroll=8)
        here = slice(c * part, (c + 1) * part)
        copies.append(pltpu.make_async_copy(stage.at[here, :], out.at[here, :], sems.at[c]))
        copies[-1].start()
    for copy in copies:
        copy.wait()


def finish(stats, gain, bias, resp, occ, population):
    channels, tile_rows = resp.shape
    whole = pl.BlockSpec(memory_space=pltpu.VMEM)
    return pl.pallas_call(
        functools.partial(finish_kernel, population),
        in_specs=[whole] * 5,
        out_specs=pl.BlockSpec(memory_space=pl.ANY),
        out_shape=jax.ShapeDtypeStruct((tile_rows, channels), BF16),
        scratch_shapes=[pltpu.VMEM((tile_rows, channels), BF16), pltpu.SemaphoreType.DMA((8,))],
        compiler_params=pltpu.CompilerParams(vmem_limit_bytes=16 * MIB),
        name="finish",
    )(stats, gain.reshape(1, channels), bias.reshape(1, channels), resp, occ)


def shards(voxels, owner_tile, rim_blocks, kernel_map, weights, norm_gain, shift_bias):
    devices = lax.axis_size(AXES)
    offsets, tile_rows = kernel_map.shape[1:]
    pair_rows = tile_rows // devices
    block = pair_rows
    channels = voxels.shape[1]

    def swap(value):
        return lax.all_to_all(value, AXES, split_axis=0, concat_axis=0, tiled=True)

    odd_row, odd_col = lax.axis_index("tx") % 2, lax.axis_index("ty") % 2
    ways = jnp.stack((odd_row, 1 - odd_row, 2 + odd_col, 3 - odd_col)).astype(I32)
    outgoing = place(voxels, owner_tile, tile_rows, pair_rows)
    ways, outgoing = lax.optimization_barrier((ways, outgoing))
    arrival = swap(outgoing.reshape(devices, pair_rows, channels)).reshape(tile_rows, channels)
    kmap = kernel_map.transpose(1, 0, 2)
    source = source_blocks(kmap, block)
    picked = pick(arrival, rim_blocks[0], ways, block)
    rims = (
        exchanged(picked[0], "tx", 0),
        exchanged(picked[1], "tx", 1),
        exchanged(picked[2], "ty", 0),
        exchanged(picked[3], "ty", 1),
    )
    xt, occ, weights_t = turn_local(arrival, weights, block)
    resp, stats = convolve(source, ways, kmap, xt, rims, weights_t, occ, block)
    gathered = swap(stats)
    return finish(gathered, norm_gain, shift_bias, resp, occ, float(voxels.shape[0] * devices))


def solution(mesh):
    return jax.shard_map(
        shards,
        mesh=mesh,
        in_specs=(
            P(AXES, None),
            P(AXES, None),
            P(AXES, None, None),
            P(AXES, None, None),
            P(),
            P(),
            P(),
        ),
        out_specs=P(AXES, None),
        check_vma=False,
    )
```

```python
import functools

import jax
import jax.numpy as jnp
from jax import lax
from jax.experimental import pallas as pl
from jax.experimental.pallas import tpu as pltpu
from jax.sharding import PartitionSpec as P

AXES = ("tx", "ty")
LANES = 128
BF16, F32, I32, I16 = jnp.bfloat16, jnp.float32, jnp.int32, jnp.int16
EMPTY = -1.0
MIB = 1 << 20
REGION = 8
LANE_TURN = 6


def exchanged(value, axis, first):
    pairs = range(first, lax.axis_size(axis) - 1, 2)
    return lax.ppermute(value, axis, [way for i in pairs for way in ((i, i + 1), (i + 1, i))])


def place_kernel(pair_rows, owner, voxels, out, held, addr_v, addr_s, wide, slots, sems):
    rows = voxels.shape[0]
    tiles = out.shape[0] // pair_rows
    fetch = pltpu.make_async_copy(voxels, held, sems.at[0])
    fetch.start()
    run_len = min(512, rows)
    earlier = lax.broadcasted_iota(I32, (run_len, run_len), 0)
    later = lax.broadcasted_iota(I32, (run_len, run_len), 1)
    upto = (earlier <= later).astype(BF16)
    tile_ids = lax.broadcasted_iota(I32, (tiles, run_len), 0)
    before = jnp.zeros((tiles, 1), F32)
    for first in range(0, rows, run_len):
        target = owner[:, first : first + run_len]
        member = tile_ids == target
        inside = jnp.dot(member.astype(BF16), upto, preferred_element_type=F32) + before
        rank = jnp.sum(jnp.where(member, inside, 0.0), axis=0, keepdims=True)
        address = target * pair_rows + rank.astype(I32) - 1
        for j in range(0, run_len, LANES):
            line = (first + j) // LANES
            addr_v[line : line + 1, :] = address[:, j : j + LANES]
        before = inside[:, run_len - 1 : run_len]
    copy = pltpu.make_async_copy(addr_v, addr_s, sems.at[1])
    copy.start()
    chunk = 256

    @pl.loop(0, out.shape[0] // chunk)
    def _(i):
        here = pl.ds(pl.multiple_of(i * chunk, chunk), chunk)
        slots[here, :] = jnp.full((chunk, slots.shape[1]), EMPTY, F32)

    fetch.wait()

    @pl.loop(0, rows // chunk)
    def _(i):
        here = pl.ds(pl.multiple_of(i * chunk, chunk), chunk)
        wide[here, :] = held[here, :].astype(F32)

    copy.wait()

    lines = rows // LANES
    for first in range(0, lines, REGION):

        @pl.when(addr_s[first, 0] >= 0)
        def _():
            for line in range(first, min(first + REGION, lines)):
                for u in range(LANES):
                    row = line * LANES + u
                    slots[pl.ds(addr_s[line, u], 1), :] = wide[row : row + 1, :]

    @pl.loop(0, out.shape[0] // chunk)
    def _(i):
        here = pl.ds(pl.multiple_of(i * chunk, chunk), chunk)
        out[here, :] = slots[here, :].astype(BF16)


def place(voxels, owner_tile, tile_rows, pair_rows):
    rows, channels = voxels.shape
    return pl.pallas_call(
        functools.partial(place_kernel, pair_rows),
        in_specs=[pl.BlockSpec(memory_space=pltpu.VMEM), pl.BlockSpec(memory_space=pl.ANY)],
        out_specs=pl.BlockSpec(memory_space=pltpu.VMEM),
        out_shape=jax.ShapeDtypeStruct((tile_rows, channels), BF16),
        scratch_shapes=[
            pltpu.VMEM((rows, channels), BF16),
            pltpu.VMEM((rows // LANES, LANES), I32),
            pltpu.SMEM((rows // LANES, LANES), I32),
            pltpu.VMEM((rows, channels), F32),
            pltpu.VMEM((tile_rows, channels), F32),
            pltpu.SemaphoreType.DMA((2,)),
        ],
        compiler_params=pltpu.CompilerParams(vmem_limit_bytes=32 * MIB),
        name="place",
    )(owner_tile.T, voxels)


def pick_kernel(block, listed, ways, arrival, *outs):
    count = outs[0].shape[0] // block
    for d, out in enumerate(outs):
        for i in range(count):
            at = pl.multiple_of(listed[ways[d], i] * block, block)
            out[i * block : (i + 1) * block, :] = arrival[pl.ds(at, block), :]


def pick(arrival, listed, ways, block):
    directions, count = listed.shape
    shape = jax.ShapeDtypeStruct((count * block, arrival.shape[1]), arrival.dtype)
    return pl.pallas_call(
        functools.partial(pick_kernel, block),
        in_specs=[
            pl.BlockSpec(memory_space=pltpu.SMEM),
            pl.BlockSpec(memory_space=pltpu.SMEM),
            pl.BlockSpec(memory_space=pltpu.VMEM),
        ],
        out_specs=[pl.BlockSpec(memory_space=pltpu.VMEM)] * directions,
        out_shape=[shape] * directions,
        compiler_params=pltpu.CompilerParams(vmem_limit_bytes=16 * MIB),
        name="pick_rims",
    )(listed, ways, arrival)


def source_kernel(block, kmap, out):
    offsets, tile_rows = kmap.shape[0], kmap.shape[2]
    lane = lax.broadcasted_iota(I32, (offsets, LANES), 1)
    right = lane >= block
    found = jnp.zeros((offsets, LANES), I32)
    for p in range(tile_rows // LANES):
        listed = kmap[:, 0, p * LANES : (p + 1) * LANES]
        for half, mine in enumerate((jnp.logical_not(right), right)):
            top = jnp.max(jnp.where(mine, listed, 0), axis=1, keepdims=True)
            found = jnp.where(lane == 2 * p + half, top, found)
    out[...] = found // block


def source_blocks(kmap, block):
    offsets, _, tile_rows = kmap.shape
    return pl.pallas_call(
        functools.partial(source_kernel, block),
        out_shape=jax.ShapeDtypeStruct((offsets, tile_rows // block), I32),
        compiler_params=pltpu.CompilerParams(vmem_limit_bytes=16 * MIB),
        name="source_blocks",
    )(kmap)


def lane_gather(value, index):
    numbers = lax.GatherDimensionNumbers(
        offset_dims=(),
        collapsed_slice_dims=(1,),
        start_index_map=(1,),
        operand_batching_dims=(0,),
        start_indices_batching_dims=(0,),
    )
    mode = lax.GatherScatterMode.PROMISE_IN_BOUNDS
    return lax.gather(value, index[..., None], numbers, (1, 1), mode=mode)


def same_of(channels):
    row = lax.broadcasted_iota(I32, (channels, channels), 0)
    lane = lax.broadcasted_iota(I32, (channels, channels), 1)
    return (row == lane).astype(BF16)


def turned(same, rows):
    return lax.dot_general(same, rows, (((1,), (1,)), ((), ())), preferred_element_type=F32)


def turn_pair(same, part, p, block):
    straight = part[pl.ds(pl.multiple_of(p * LANES, LANES), LANES), :]
    swapped = jnp.concatenate((straight[block:], straight[:block]), axis=0)
    return turned(same, jnp.concatenate((straight, swapped), axis=0))


def turn_kernel(block, arrival, weights, xt, occ, weights_t):
    channels = arrival.shape[1]
    same = same_of(channels)

    def turn(p, carry):
        both = turn_pair(same, arrival, p, block)
        occ[:, pl.ds(pl.multiple_of(p * LANES, LANES), LANES)] = (both[0:1, :LANES] >= 0.0).astype(F32)
        both = jnp.maximum(both, 0.0).astype(BF16)
        xt[2 * p] = both[:, :LANES]
        xt[2 * p + 1] = both[:, LANES:]
        return carry

    lax.fori_loop(0, arrival.shape[0] // LANES, turn, 0, unroll=8)
    for k in range(weights.shape[0]):
        weights_t[:, k * channels : (k + 1) * channels] = turned(same, weights[k]).astype(BF16)


def turn_local(arrival, weights, block):
    tile_rows, channels = arrival.shape
    offsets = weights.shape[0]
    return pl.pallas_call(
        functools.partial(turn_kernel, block),
        out_shape=[
            jax.ShapeDtypeStruct((tile_rows // block, channels, LANES), BF16),
            jax.ShapeDtypeStruct((1, tile_rows), F32),
            jax.ShapeDtypeStruct((weights.shape[2], offsets * channels), BF16),
        ],
        compiler_params=pltpu.CompilerParams(vmem_limit_bytes=16 * MIB),
        name="turn_local",
    )(arrival, weights)


def conv_kernel(block, window, source, ways, kmap, xt_local, rim0, rim1, rim2, rim3, weights_t, occ, resp, stats, xt, g):
    offsets, tile_rows = kmap.shape[0], kmap.shape[2]
    channels = xt_local.shape[1]
    same = same_of(channels)
    lane = lax.broadcasted_iota(I32, (channels, LANES), 1)
    right = lane >= block
    half = jnp.where(lax.broadcasted_iota(I32, (1, LANES), 1) >= block, block, 0)
    rows16 = lax.broadcasted_iota(I32, (LANES, LANES), 0).astype(I16)
    none = jnp.zeros((LANES, LANES), BF16)

    def keep(i, carry):
        xt[i] = xt_local[i]
        return carry

    local_blocks = xt_local.shape[0]
    lax.fori_loop(0, local_blocks, keep, 0, unroll=8)
    for d, part in enumerate((rim0, rim1, rim2, rim3)):
        first = local_blocks + (ways[d] ^ 1) * (part.shape[0] // block)

        def turn(p, carry, part=part, first=first):
            both = jnp.maximum(turn_pair(same, part, p, block), 0.0).astype(BF16)
            xt[first + 2 * p] = both[:, :LANES]
            xt[first + 2 * p + 1] = both[:, LANES:]
            return carry

        lax.fori_loop(0, part.shape[0] // LANES, turn, 0, unroll=8)

    blocks = window // block

    def convolve_window(step, total):
        def pair_of(k, p):
            left_block = source[k, blocks * step + 2 * p]
            right_block = source[k, blocks * step + 2 * p + 1]
            return jnp.where(right, xt[right_block ^ 1], xt[left_block])

        def chooser_of(k, p):
            at = pl.ds(pl.multiple_of(step * window, window) + p * LANES, LANES)
            listed = kmap[k, :, at]
            local = jnp.where(listed < 0, -1, (listed & (block - 1)) + half)
            local = jnp.broadcast_to(local, (LANES, LANES)).astype(I16)
            return jnp.where(rows16 == local, jnp.ones((), BF16), jnp.zeros((), BF16))

        for k in range(offsets):
            for p in range(0, window // LANES, 2):
                to = slice(k * channels, (k + 1) * channels)
                if k == offsets // 2:
                    for q in (p, p + 1):
                        g[to, q * LANES : (q + 1) * LANES] = xt[blocks * step + 2 * q]
                    continue
                if k % LANE_TURN == 0:
                    for q in (p, p + 1):
                        at = pl.ds(pl.multiple_of(step * window, window) + q * LANES, LANES)
                        listed = kmap[k, :, at]
                        index = jnp.broadcast_to((listed & (block - 1)) + half, (channels, LANES)).astype(I16)
                        there = jnp.broadcast_to(listed, (channels, LANES)).astype(I16) >= 0
                        chosen = jnp.where(there, lane_gather(pair_of(k, q), index), jnp.zeros((), BF16))
                        g[to, q * LANES : (q + 1) * LANES] = chosen
                    continue
                pairs = jnp.concatenate((pair_of(k, p), pair_of(k, p + 1)), axis=1)
                chooser = jnp.concatenate(
                    (
                        jnp.concatenate((chooser_of(k, p), none), axis=1),
                        jnp.concatenate((none, chooser_of(k, p + 1)), axis=1),
                    ),
                    axis=0,
                )
                chosen = jnp.dot(pairs, chooser, preferred_element_type=F32).astype(BF16)
                g[to, p * LANES : (p + 2) * LANES] = chosen
        here = pl.ds(pl.multiple_of(step * window, window), window)
        value = jnp.dot(weights_t[...], g[...], preferred_element_type=F32) * occ[:, here]
        resp[:, here] = value
        for p in range(window // LANES):
            total = total + value[:, p * LANES : (p + 1) * LANES]
        return total

    zero = jnp.zeros((channels, LANES), F32)
    total = lax.fori_loop(0, tile_rows // window, convolve_window, zero)
    total = jnp.sum(total, axis=1, keepdims=True)
    number = jnp.sum(occ[...], axis=1, keepdims=True)
    mean = total / jnp.maximum(number, 1.0)

    def spread(p, squares):
        at = pl.ds(pl.multiple_of(p * LANES, LANES), LANES)
        centred = (resp[:, at] - mean) * occ[:, at]
        return squares + centred * centred

    squares = lax.fori_loop(0, tile_rows // LANES, spread, zero, unroll=4)
    squares = jnp.sum(squares, axis=1, keepdims=True)
    columns = jnp.where(lane == 0, total, jnp.where(lane == 1, squares, jnp.broadcast_to(number, (channels, LANES))))
    lines = columns.T
    line = jnp.concatenate((lines[0:1], lines[1:2], lines[2:3]), axis=1)

    def tell(i, carry):
        stats[i] = line
        return carry

    lax.fori_loop(0, stats.shape[0], tell, 0, unroll=8)


def convolve(source, ways, kmap, xt_local, rims, weights_t, occ, block):
    offsets, _, tile_rows = kmap.shape
    local_blocks, channels, _ = xt_local.shape
    window = min(1024, tile_rows)
    ext_blocks = local_blocks + sum(rim.shape[0] for rim in rims) // block
    whole = pl.BlockSpec(memory_space=pltpu.VMEM)
    return pl.pallas_call(
        functools.partial(conv_kernel, block, window),
        in_specs=[pl.BlockSpec(memory_space=pltpu.SMEM)] * 2 + [whole] * 8,
        out_specs=[whole, whole],
        out_shape=[
            jax.ShapeDtypeStruct((channels, tile_rows), F32),
            jax.ShapeDtypeStruct((tile_rows // block, 1, 3 * channels), F32),
        ],
        scratch_shapes=[
            pltpu.VMEM((ext_blocks, channels, LANES), BF16),
            pltpu.VMEM((offsets * channels, window), BF16),
        ],
        compiler_params=pltpu.CompilerParams(vmem_limit_bytes=40 * MIB),
        name="convolve",
    )(source, ways, kmap, xt_local, *rims, weights_t, occ)


def finish_kernel(population, stats, gain, bias, resp, occ, out, stage, sems):
    channels, tile_rows = resp.shape
    total = stats[:, 0, :channels]
    squares = stats[:, 0, channels : 2 * channels]
    number = stats[:, 0, 2 * channels :]
    average = jnp.sum(total, axis=0, keepdims=True) / population
    apart = total / jnp.maximum(number, 1.0) - average
    spread = jnp.sum(squares + number * apart * apart, axis=0, keepdims=True)
    scale = gain[...] / jnp.sqrt(spread / population + 1e-05)
    row = lax.broadcasted_iota(I32, (LANES, channels), 0)
    affine = jnp.where(row == 0, average, jnp.where(row == 1, scale, bias[...])).T
    average, scale, shift = affine[:, 0:1], affine[:, 1:2], affine[:, 2:3]
    count = sems.shape[0]
    part = tile_rows // count
    copies = []
    for c in range(count):

        def turn(p, carry, c=c):
            at = pl.ds(pl.multiple_of(c * part + p * LANES, LANES), LANES)
            value = jnp.maximum((resp[:, at] - average) * scale + shift, 0.0) * occ[:, at]
            stage[at, :] = value.T.astype(BF16)
            return carry

        lax.fori_loop(0, part // LANES, turn, 0, unroll=8)
        here = slice(c * part, (c + 1) * part)
        copies.append(pltpu.make_async_copy(stage.at[here, :], out.at[here, :], sems.at[c]))
        copies[-1].start()
    for copy in copies:
        copy.wait()


def finish(stats, gain, bias, resp, occ, population):
    channels, tile_rows = resp.shape
    whole = pl.BlockSpec(memory_space=pltpu.VMEM)
    return pl.pallas_call(
        functools.partial(finish_kernel, population),
        in_specs=[whole] * 5,
        out_specs=pl.BlockSpec(memory_space=pl.ANY),
        out_shape=jax.ShapeDtypeStruct((tile_rows, channels), BF16),
        scratch_shapes=[pltpu.VMEM((tile_rows, channels), BF16), pltpu.SemaphoreType.DMA((8,))],
        compiler_params=pltpu.CompilerParams(vmem_limit_bytes=16 * MIB),
        name="finish",
    )(stats, gain.reshape(1, channels), bias.reshape(1, channels), resp, occ)


def shards(voxels, owner_tile, rim_blocks, kernel_map, weights, norm_gain, shift_bias):
    devices = lax.axis_size(AXES)
    offsets, tile_rows = kernel_map.shape[1:]
    pair_rows = tile_rows // devices
    block = pair_rows
    channels = voxels.shape[1]

    def swap(value):
        return lax.all_to_all(value, AXES, split_axis=0, concat_axis=0, tiled=True)

    odd_row, odd_col = lax.axis_index("tx") % 2, lax.axis_index("ty") % 2
    ways = jnp.stack((odd_row, 1 - odd_row, 2 + odd_col, 3 - odd_col)).astype(I32)
    outgoing = place(voxels, owner_tile, tile_rows, pair_rows)
    ways, outgoing = lax.optimization_barrier((ways, outgoing))
    arrival = swap(outgoing.reshape(devices, pair_rows, channels)).reshape(tile_rows, channels)
    kmap = kernel_map.transpose(1, 0, 2)
    source = source_blocks(kmap, block)
    picked = pick(arrival, rim_blocks[0], ways, block)
    rims = (
        exchanged(picked[0], "tx", 0),
        exchanged(picked[1], "tx", 1),
        exchanged(picked[2], "ty", 0),
        exchanged(picked[3], "ty", 1),
    )
    xt, occ, weights_t = turn_local(arrival, weights, block)
    resp, stats = convolve(source, ways, kmap, xt, rims, weights_t, occ, block)
    gathered = swap(stats)
    return finish(gathered, norm_gain, shift_bias, resp, occ, float(voxels.shape[0] * devices))


def solution(mesh):
    return jax.shard_map(
        shards,
        mesh=mesh,
        in_specs=(
            P(AXES, None),
            P(AXES, None),
            P(AXES, None, None),
            P(AXES, None, None),
            P(),
            P(),
            P(),
        ),
        out_specs=P(AXES, None),
        check_vma=False,
    )
```

```python
import functools

import jax
import jax.numpy as jnp
from jax import lax
from jax.experimental import pallas as pl
from jax.experimental.pallas import tpu as pltpu
from jax.sharding import PartitionSpec as P

AXES = ("tx", "ty")
LANES = 128
BF16, F32, I32, I16 = jnp.bfloat16, jnp.float32, jnp.int32, jnp.int16
EMPTY = -1.0
MIB = 1 << 20
REGION = 8
LANE_TURN = 6


def exchanged(value, axis, first):
    pairs = range(first, lax.axis_size(axis) - 1, 2)
    return lax.ppermute(value, axis, [way for i in pairs for way in ((i, i + 1), (i + 1, i))])


def place_kernel(pair_rows, owner, voxels, out, held, addr_v, addr_s, wide, slots, sems):
    rows = voxels.shape[0]
    tiles = out.shape[0] // pair_rows
    fetch = pltpu.make_async_copy(voxels, held, sems.at[0])
    fetch.start()
    run_len = min(512, rows)
    earlier = lax.broadcasted_iota(I32, (run_len, run_len), 0)
    later = lax.broadcasted_iota(I32, (run_len, run_len), 1)
    upto = (earlier <= later).astype(BF16)
    tile_ids = lax.broadcasted_iota(I32, (tiles, run_len), 0)
    before = jnp.zeros((tiles, 1), F32)
    for first in range(0, rows, run_len):
        target = owner[:, first : first + run_len]
        member = tile_ids == target
        inside = jnp.dot(member.astype(BF16), upto, preferred_element_type=F32) + before
        rank = jnp.sum(jnp.where(member, inside, 0.0), axis=0, keepdims=True)
        address = target * pair_rows + rank.astype(I32) - 1
        for j in range(0, run_len, LANES):
            line = (first + j) // LANES
            addr_v[line : line + 1, :] = address[:, j : j + LANES]
        before = inside[:, run_len - 1 : run_len]
    copy = pltpu.make_async_copy(addr_v, addr_s, sems.at[1])
    copy.start()
    chunk = 256

    @pl.loop(0, out.shape[0] // chunk)
    def _(i):
        here = pl.ds(pl.multiple_of(i * chunk, chunk), chunk)
        slots[here, :] = jnp.full((chunk, slots.shape[1]), EMPTY, F32)

    fetch.wait()

    @pl.loop(0, rows // chunk)
    def _(i):
        here = pl.ds(pl.multiple_of(i * chunk, chunk), chunk)
        wide[here, :] = held[here, :].astype(F32)

    copy.wait()

    lines = rows // LANES
    for first in range(0, lines, REGION):

        @pl.when(addr_s[first, 0] >= 0)
        def _():
            for line in range(first, min(first + REGION, lines)):
                for u in range(LANES):
                    row = line * LANES + u
                    slots[pl.ds(addr_s[line, u], 1), :] = wide[row : row + 1, :]

    @pl.loop(0, out.shape[0] // chunk)
    def _(i):
        here = pl.ds(pl.multiple_of(i * chunk, chunk), chunk)
        out[here, :] = slots[here, :].astype(BF16)


def place(voxels, owner_tile, tile_rows, pair_rows):
    rows, channels = voxels.shape
    return pl.pallas_call(
        functools.partial(place_kernel, pair_rows),
        in_specs=[pl.BlockSpec(memory_space=pltpu.VMEM), pl.BlockSpec(memory_space=pl.ANY)],
        out_specs=pl.BlockSpec(memory_space=pltpu.VMEM),
        out_shape=jax.ShapeDtypeStruct((tile_rows, channels), BF16),
        scratch_shapes=[
            pltpu.VMEM((rows, channels), BF16),
            pltpu.VMEM((rows // LANES, LANES), I32),
            pltpu.SMEM((rows // LANES, LANES), I32),
            pltpu.VMEM((rows, channels), F32),
            pltpu.VMEM((tile_rows, channels), F32),
            pltpu.SemaphoreType.DMA((2,)),
        ],
        compiler_params=pltpu.CompilerParams(vmem_limit_bytes=32 * MIB),
        name="place",
    )(owner_tile.T, voxels)


def pick_kernel(block, listed, ways, arrival, *outs):
    count = outs[0].shape[0] // block
    for d, out in enumerate(outs):
        for i in range(count):
            at = pl.multiple_of(listed[ways[d], i] * block, block)
            out[i * block : (i + 1) * block, :] = arrival[pl.ds(at, block), :]


def pick(arrival, listed, ways, block):
    directions, count = listed.shape
    shape = jax.ShapeDtypeStruct((count * block, arrival.shape[1]), arrival.dtype)
    return pl.pallas_call(
        functools.partial(pick_kernel, block),
        in_specs=[
            pl.BlockSpec(memory_space=pltpu.SMEM),
            pl.BlockSpec(memory_space=pltpu.SMEM),
            pl.BlockSpec(memory_space=pltpu.VMEM),
        ],
        out_specs=[pl.BlockSpec(memory_space=pltpu.VMEM)] * directions,
        out_shape=[shape] * directions,
        compiler_params=pltpu.CompilerParams(vmem_limit_bytes=16 * MIB),
        name="pick_rims",
    )(listed, ways, arrival)


def source_kernel(block, kmap, out):
    offsets, pairs, _ = kmap.shape
    lane = lax.broadcasted_iota(I32, (pairs, LANES), 1)
    right = lane >= block
    found = jnp.zeros((pairs, LANES), I32)
    for k in range(offsets):
        listed = kmap[k]
        for half, mine in enumerate((jnp.logical_not(right), right)):
            top = jnp.max(jnp.where(mine, listed, 0), axis=1, keepdims=True)
            found = jnp.where(lane == 2 * k + half, top, found)
    out[...] = found // block


def source_blocks(kmap, block):
    offsets, _, tile_rows = kmap.shape
    pairs = tile_rows // LANES
    return pl.pallas_call(
        functools.partial(source_kernel, block),
        out_shape=jax.ShapeDtypeStruct((pairs, LANES), I32),
        compiler_params=pltpu.CompilerParams(vmem_limit_bytes=16 * MIB),
        name="source_blocks",
    )(kmap.reshape(offsets, pairs, LANES))


def lane_gather(value, index):
    numbers = lax.GatherDimensionNumbers(
        offset_dims=(),
        collapsed_slice_dims=(1,),
        start_index_map=(1,),
        operand_batching_dims=(0,),
        start_indices_batching_dims=(0,),
    )
    mode = lax.GatherScatterMode.PROMISE_IN_BOUNDS
    return lax.gather(value, index[..., None], numbers, (1, 1), mode=mode)


def same_of(channels):
    row = lax.broadcasted_iota(I32, (channels, channels), 0)
    lane = lax.broadcasted_iota(I32, (channels, channels), 1)
    return (row == lane).astype(BF16)


def turned(same, rows):
    return lax.dot_general(same, rows, (((1,), (1,)), ((), ())), preferred_element_type=F32)


def turn_pair(same, part, p, block):
    straight = part[pl.ds(pl.multiple_of(p * LANES, LANES), LANES), :]
    swapped = jnp.concatenate((straight[block:], straight[:block]), axis=0)
    return turned(same, jnp.concatenate((straight, swapped), axis=0))


def turn_kernel(block, arrival, weights, xt, occ, weights_t):
    channels = arrival.shape[1]
    same = same_of(channels)

    def turn(p, carry):
        both = turn_pair(same, arrival, p, block)
        occ[:, pl.ds(pl.multiple_of(p * LANES, LANES), LANES)] = (both[0:1, :LANES] >= 0.0).astype(F32)
        both = jnp.maximum(both, 0.0).astype(BF16)
        xt[2 * p] = both[:, :LANES]
        xt[2 * p + 1] = both[:, LANES:]
        return carry

    lax.fori_loop(0, arrival.shape[0] // LANES, turn, 0, unroll=16)
    for k in range(weights.shape[0]):
        weights_t[:, k * channels : (k + 1) * channels] = turned(same, weights[k]).astype(BF16)


def turn_local(arrival, weights, block):
    tile_rows, channels = arrival.shape
    offsets = weights.shape[0]
    return pl.pallas_call(
        functools.partial(turn_kernel, block),
        out_shape=[
            jax.ShapeDtypeStruct((tile_rows // block, channels, LANES), BF16),
            jax.ShapeDtypeStruct((1, tile_rows), F32),
            jax.ShapeDtypeStruct((weights.shape[2], offsets * channels), BF16),
        ],
        compiler_params=pltpu.CompilerParams(vmem_limit_bytes=16 * MIB),
        name="turn_local",
    )(arrival, weights)


def conv_kernel(block, window, source, ways, kmap, xt_local, rim0, rim1, rim2, rim3, weights_t, occ, resp, stats, xt, g):
    offsets, tile_rows = kmap.shape[0], kmap.shape[2]
    channels = xt_local.shape[1]
    same = same_of(channels)
    lane = lax.broadcasted_iota(I32, (channels, LANES), 1)
    right = lane >= block
    half = jnp.where(lax.broadcasted_iota(I32, (1, LANES), 1) >= block, block, 0)
    rows16 = lax.broadcasted_iota(I32, (LANES, LANES), 0).astype(I16)
    none = jnp.zeros((LANES, LANES), BF16)

    def keep(i, carry):
        xt[i] = xt_local[i]
        return carry

    local_blocks = xt_local.shape[0]
    lax.fori_loop(0, local_blocks, keep, 0, unroll=8)
    for d, part in enumerate((rim0, rim1, rim2, rim3)):
        first = local_blocks + (ways[d] ^ 1) * (part.shape[0] // block)

        def turn(p, carry, part=part, first=first):
            both = jnp.maximum(turn_pair(same, part, p, block), 0.0).astype(BF16)
            xt[first + 2 * p] = both[:, :LANES]
            xt[first + 2 * p + 1] = both[:, LANES:]
            return carry

        lax.fori_loop(0, part.shape[0] // LANES, turn, 0, unroll=8)

    blocks = window // block

    def convolve_window(step, total):
        def pair_of(k, p):
            line = blocks // 2 * step + p
            left_block = source[line, 2 * k]
            right_block = source[line, 2 * k + 1]
            return jnp.where(right, xt[right_block ^ 1], xt[left_block])

        def chooser_of(k, p):
            at = pl.ds(pl.multiple_of(step * window, window) + p * LANES, LANES)
            listed = kmap[k, :, at]
            local = jnp.where(listed < 0, -1, (listed & (block - 1)) + half)
            local = jnp.broadcast_to(local, (LANES, LANES)).astype(I16)
            return jnp.where(rows16 == local, jnp.ones((), BF16), jnp.zeros((), BF16))

        for k in range(offsets):
            for p in range(0, window // LANES, 2):
                to = slice(k * channels, (k + 1) * channels)
                if k == offsets // 2:
                    for q in (p, p + 1):
                        g[to, q * LANES : (q + 1) * LANES] = xt[blocks * step + 2 * q]
                    continue
                if k % LANE_TURN == 0:
                    for q in (p, p + 1):
                        at = pl.ds(pl.multiple_of(step * window, window) + q * LANES, LANES)
                        listed = kmap[k, :, at]
                        index = jnp.broadcast_to((listed & (block - 1)) + half, (channels, LANES)).astype(I16)
                        there = jnp.broadcast_to(listed, (channels, LANES)).astype(I16) >= 0
                        chosen = jnp.where(there, lane_gather(pair_of(k, q), index), jnp.zeros((), BF16))
                        g[to, q * LANES : (q + 1) * LANES] = chosen
                    continue
                pairs = jnp.concatenate((pair_of(k, p), pair_of(k, p + 1)), axis=1)
                chooser = jnp.concatenate(
                    (
                        jnp.concatenate((chooser_of(k, p), none), axis=1),
                        jnp.concatenate((none, chooser_of(k, p + 1)), axis=1),
                    ),
                    axis=0,
                )
                chosen = jnp.dot(pairs, chooser, preferred_element_type=F32).astype(BF16)
                g[to, p * LANES : (p + 2) * LANES] = chosen
        here = pl.ds(pl.multiple_of(step * window, window), window)
        value = jnp.dot(weights_t[...], g[...], preferred_element_type=F32) * occ[:, here]
        resp[:, here] = value
        for p in range(window // LANES):
            total = total + value[:, p * LANES : (p + 1) * LANES]
        return total

    zero = jnp.zeros((channels, LANES), F32)
    total = lax.fori_loop(0, tile_rows // window, convolve_window, zero)
    total = jnp.sum(total, axis=1, keepdims=True)
    number = jnp.sum(occ[...], axis=1, keepdims=True)
    mean = total / jnp.maximum(number, 1.0)

    def spread(p, squares):
        at = pl.ds(pl.multiple_of(p * LANES, LANES), LANES)
        centred = (resp[:, at] - mean) * occ[:, at]
        return squares + centred * centred

    squares = lax.fori_loop(0, tile_rows // LANES, spread, zero, unroll=4)
    squares = jnp.sum(squares, axis=1, keepdims=True)
    columns = jnp.where(lane == 0, total, jnp.where(lane == 1, squares, jnp.broadcast_to(number, (channels, LANES))))
    lines = columns.T
    line = jnp.concatenate((lines[0:1], lines[1:2], lines[2:3]), axis=1)

    def tell(i, carry):
        stats[i] = line
        return carry

    lax.fori_loop(0, stats.shape[0], tell, 0, unroll=8)


def convolve(source, ways, kmap, xt_local, rims, weights_t, occ, block):
    offsets, _, tile_rows = kmap.shape
    local_blocks, channels, _ = xt_local.shape
    window = min(1024, tile_rows)
    ext_blocks = local_blocks + sum(rim.shape[0] for rim in rims) // block
    whole = pl.BlockSpec(memory_space=pltpu.VMEM)
    return pl.pallas_call(
        functools.partial(conv_kernel, block, window),
        in_specs=[pl.BlockSpec(memory_space=pltpu.SMEM)] * 2 + [whole] * 8,
        out_specs=[whole, whole],
        out_shape=[
            jax.ShapeDtypeStruct((channels, tile_rows), F32),
            jax.ShapeDtypeStruct((tile_rows // block, 1, 3 * channels), F32),
        ],
        scratch_shapes=[
            pltpu.VMEM((ext_blocks, channels, LANES), BF16),
            pltpu.VMEM((offsets * channels, window), BF16),
        ],
        compiler_params=pltpu.CompilerParams(vmem_limit_bytes=40 * MIB),
        name="convolve",
    )(source, ways, kmap, xt_local, *rims, weights_t, occ)


def finish_kernel(population, stats, gain, bias, resp, occ, out, stage, sems):
    channels, tile_rows = resp.shape
    total = stats[:, 0, :channels]
    squares = stats[:, 0, channels : 2 * channels]
    number = stats[:, 0, 2 * channels :]
    average = jnp.sum(total, axis=0, keepdims=True) / population
    apart = total / jnp.maximum(number, 1.0) - average
    spread = jnp.sum(squares + number * apart * apart, axis=0, keepdims=True)
    scale = gain[...] / jnp.sqrt(spread / population + 1e-05)
    row = lax.broadcasted_iota(I32, (LANES, channels), 0)
    affine = jnp.where(row == 0, average, jnp.where(row == 1, scale, bias[...])).T
    average, scale, shift = affine[:, 0:1], affine[:, 1:2], affine[:, 2:3]
    count = sems.shape[0]
    part = tile_rows // count
    copies = []
    for c in range(count):

        def turn(p, carry, c=c):
            at = pl.ds(pl.multiple_of(c * part + p * LANES, LANES), LANES)
            value = jnp.maximum((resp[:, at] - average) * scale + shift, 0.0) * occ[:, at]
            stage[at, :] = value.T.astype(BF16)
            return carry

        lax.fori_loop(0, part // LANES, turn, 0, unroll=8)
        here = slice(c * part, (c + 1) * part)
        copies.append(pltpu.make_async_copy(stage.at[here, :], out.at[here, :], sems.at[c]))
        copies[-1].start()
    for copy in copies:
        copy.wait()


def finish(stats, gain, bias, resp, occ, population):
    channels, tile_rows = resp.shape
    whole = pl.BlockSpec(memory_space=pltpu.VMEM)
    return pl.pallas_call(
        functools.partial(finish_kernel, population),
        in_specs=[whole] * 5,
        out_specs=pl.BlockSpec(memory_space=pl.ANY),
        out_shape=jax.ShapeDtypeStruct((tile_rows, channels), BF16),
        scratch_shapes=[pltpu.VMEM((tile_rows, channels), BF16), pltpu.SemaphoreType.DMA((8,))],
        compiler_params=pltpu.CompilerParams(vmem_limit_bytes=16 * MIB),
        name="finish",
    )(stats, gain.reshape(1, channels), bias.reshape(1, channels), resp, occ)


def shards(voxels, owner_tile, rim_blocks, kernel_map, weights, norm_gain, shift_bias):
    devices = lax.axis_size(AXES)
    offsets, tile_rows = kernel_map.shape[1:]
    pair_rows = tile_rows // devices
    block = pair_rows
    channels = voxels.shape[1]

    def swap(value):
        return lax.all_to_all(value, AXES, split_axis=0, concat_axis=0, tiled=True)

    odd_row, odd_col = lax.axis_index("tx") % 2, lax.axis_index("ty") % 2
    ways = jnp.stack((odd_row, 1 - odd_row, 2 + odd_col, 3 - odd_col)).astype(I32)
    outgoing = place(voxels, owner_tile, tile_rows, pair_rows)
    ways, outgoing = lax.optimization_barrier((ways, outgoing))
    arrival = swap(outgoing.reshape(devices, pair_rows, channels)).reshape(tile_rows, channels)
    kmap = kernel_map.transpose(1, 0, 2)
    source = source_blocks(kmap, block)
    picked = pick(arrival, rim_blocks[0], ways, block)
    rims = (
        exchanged(picked[0], "tx", 0),
        exchanged(picked[1], "tx", 1),
        exchanged(picked[2], "ty", 0),
        exchanged(picked[3], "ty", 1),
    )
    xt, occ, weights_t = turn_local(arrival, weights, block)
    resp, stats = convolve(source, ways, kmap, xt, rims, weights_t, occ, block)
    gathered = swap(stats)
    return finish(gathered, norm_gain, shift_bias, resp, occ, float(voxels.shape[0] * devices))


def solution(mesh):
    return jax.shard_map(
        shards,
        mesh=mesh,
        in_specs=(
            P(AXES, None),
            P(AXES, None),
            P(AXES, None, None),
            P(AXES, None, None),
            P(),
            P(),
            P(),
        ),
        out_specs=P(AXES, None),
        check_vma=False,
    )
```

```python
import functools

import jax
import jax.numpy as jnp
from jax import lax
from jax.experimental import pallas as pl
from jax.experimental.pallas import tpu as pltpu
from jax.sharding import PartitionSpec as P

AXES = ("tx", "ty")
LANES = 128
BF16, F32, I32, I16 = jnp.bfloat16, jnp.float32, jnp.int32, jnp.int16
EMPTY = -1.0
MIB = 1 << 20
REGION = 8
LANE_TURN = 6


def exchanged(value, axis, first):
    pairs = range(first, lax.axis_size(axis) - 1, 2)
    return lax.ppermute(value, axis, [way for i in pairs for way in ((i, i + 1), (i + 1, i))])


def place_kernel(pair_rows, owner, voxels, out, held, addr_v, addr_s, wide, slots, sems):
    rows = voxels.shape[0]
    tiles = out.shape[0] // pair_rows
    fetch = pltpu.make_async_copy(voxels, held, sems.at[0])
    fetch.start()
    run_len = min(512, rows)
    earlier = lax.broadcasted_iota(I32, (run_len, run_len), 0)
    later = lax.broadcasted_iota(I32, (run_len, run_len), 1)
    upto = (earlier <= later).astype(BF16)
    tile_ids = lax.broadcasted_iota(I32, (tiles, run_len), 0)
    before = jnp.zeros((tiles, 1), F32)
    for first in range(0, rows, run_len):
        target = owner[:, first : first + run_len]
        member = tile_ids == target
        inside = jnp.dot(member.astype(BF16), upto, preferred_element_type=F32) + before
        rank = jnp.sum(jnp.where(member, inside, 0.0), axis=0, keepdims=True)
        address = target * pair_rows + rank.astype(I32) - 1
        for j in range(0, run_len, LANES):
            line = (first + j) // LANES
            addr_v[line : line + 1, :] = address[:, j : j + LANES]
        before = inside[:, run_len - 1 : run_len]
    copy = pltpu.make_async_copy(addr_v, addr_s, sems.at[1])
    copy.start()
    chunk = 256

    @pl.loop(0, out.shape[0] // chunk)
    def _(i):
        here = pl.ds(pl.multiple_of(i * chunk, chunk), chunk)
        slots[here, :] = jnp.full((chunk, slots.shape[1]), EMPTY, F32)

    fetch.wait()

    @pl.loop(0, rows // chunk)
    def _(i):
        here = pl.ds(pl.multiple_of(i * chunk, chunk), chunk)
        wide[here, :] = held[here, :].astype(F32)

    copy.wait()

    lines = rows // LANES
    for first in range(0, lines, REGION):

        @pl.when(addr_s[first, 0] >= 0)
        def _():
            for line in range(first, min(first + REGION, lines)):
                for u in range(LANES):
                    row = line * LANES + u
                    slots[pl.ds(addr_s[line, u], 1), :] = wide[row : row + 1, :]

    @pl.loop(0, out.shape[0] // chunk)
    def _(i):
        here = pl.ds(pl.multiple_of(i * chunk, chunk), chunk)
        out[here, :] = slots[here, :].astype(BF16)


def place(voxels, owner_tile, tile_rows, pair_rows):
    rows, channels = voxels.shape
    return pl.pallas_call(
        functools.partial(place_kernel, pair_rows),
        in_specs=[pl.BlockSpec(memory_space=pltpu.VMEM), pl.BlockSpec(memory_space=pl.ANY)],
        out_specs=pl.BlockSpec(memory_space=pltpu.VMEM),
        out_shape=jax.ShapeDtypeStruct((tile_rows, channels), BF16),
        scratch_shapes=[
            pltpu.VMEM((rows, channels), BF16),
            pltpu.VMEM((rows // LANES, LANES), I32),
            pltpu.SMEM((rows // LANES, LANES), I32),
            pltpu.VMEM((rows, channels), F32),
            pltpu.VMEM((tile_rows, channels), F32),
            pltpu.SemaphoreType.DMA((2,)),
        ],
        compiler_params=pltpu.CompilerParams(vmem_limit_bytes=32 * MIB),
        name="place",
    )(owner_tile.T, voxels)


def pick_kernel(block, listed, ways, arrival, *outs):
    count = outs[0].shape[0] // block
    for d, out in enumerate(outs):
        for i in range(count):
            at = pl.multiple_of(listed[ways[d], i] * block, block)
            out[i * block : (i + 1) * block, :] = arrival[pl.ds(at, block), :]


def pick(arrival, listed, ways, block):
    directions, count = listed.shape
    shape = jax.ShapeDtypeStruct((count * block, arrival.shape[1]), arrival.dtype)
    return pl.pallas_call(
        functools.partial(pick_kernel, block),
        in_specs=[
            pl.BlockSpec(memory_space=pltpu.SMEM),
            pl.BlockSpec(memory_space=pltpu.SMEM),
            pl.BlockSpec(memory_space=pltpu.VMEM),
        ],
        out_specs=[pl.BlockSpec(memory_space=pltpu.VMEM)] * directions,
        out_shape=[shape] * directions,
        compiler_params=pltpu.CompilerParams(vmem_limit_bytes=16 * MIB),
        name="pick_rims",
    )(listed, ways, arrival)


def source_kernel(block, kmap, out):
    offsets, pairs, _ = kmap.shape
    lane = lax.broadcasted_iota(I32, (pairs, LANES), 1)
    right = lane >= block
    found = jnp.zeros((pairs, LANES), I32)
    for k in range(offsets):
        listed = kmap[k]
        for half, mine in enumerate((jnp.logical_not(right), right)):
            top = jnp.max(jnp.where(mine, listed, 0), axis=1, keepdims=True)
            found = jnp.where(lane == 2 * k + half, top, found)
    out[...] = found // block


def source_blocks(kmap, block):
    offsets, _, tile_rows = kmap.shape
    pairs = tile_rows // LANES
    return pl.pallas_call(
        functools.partial(source_kernel, block),
        out_shape=jax.ShapeDtypeStruct((pairs, LANES), I32),
        compiler_params=pltpu.CompilerParams(vmem_limit_bytes=16 * MIB),
        name="source_blocks",
    )(kmap.reshape(offsets, pairs, LANES))


def lane_gather(value, index):
    numbers = lax.GatherDimensionNumbers(
        offset_dims=(),
        collapsed_slice_dims=(1,),
        start_index_map=(1,),
        operand_batching_dims=(0,),
        start_indices_batching_dims=(0,),
    )
    mode = lax.GatherScatterMode.PROMISE_IN_BOUNDS
    return lax.gather(value, index[..., None], numbers, (1, 1), mode=mode)


def same_of(channels):
    row = lax.broadcasted_iota(I32, (channels, channels), 0)
    lane = lax.broadcasted_iota(I32, (channels, channels), 1)
    return (row == lane).astype(BF16)


def turned(same, rows):
    return lax.dot_general(same, rows, (((1,), (1,)), ((), ())), preferred_element_type=F32)


def turn_pair(same, part, p, block):
    straight = part[pl.ds(pl.multiple_of(p * LANES, LANES), LANES), :]
    swapped = jnp.concatenate((straight[block:], straight[:block]), axis=0)
    return turned(same, jnp.concatenate((straight, swapped), axis=0))


def turn_kernel(block, arrival, weights, xt, occ, weights_t):
    channels = arrival.shape[1]
    same = same_of(channels)

    def turn(p, carry):
        both = turn_pair(same, arrival, p, block)
        occ[:, pl.ds(pl.multiple_of(p * LANES, LANES), LANES)] = (both[0:1, :LANES] >= 0.0).astype(F32)
        both = jnp.maximum(both, 0.0).astype(BF16)
        xt[2 * p] = both[:, :LANES]
        xt[2 * p + 1] = both[:, LANES:]
        return carry

    lax.fori_loop(0, arrival.shape[0] // LANES, turn, 0, unroll=16)
    for k in range(weights.shape[0]):
        weights_t[:, k * channels : (k + 1) * channels] = turned(same, weights[k]).astype(BF16)


def turn_local(arrival, weights, block):
    tile_rows, channels = arrival.shape
    offsets = weights.shape[0]
    return pl.pallas_call(
        functools.partial(turn_kernel, block),
        out_shape=[
            jax.ShapeDtypeStruct((tile_rows // block, channels, LANES), BF16),
            jax.ShapeDtypeStruct((1, tile_rows), F32),
            jax.ShapeDtypeStruct((weights.shape[2], offsets * channels), BF16),
        ],
        compiler_params=pltpu.CompilerParams(vmem_limit_bytes=16 * MIB),
        name="turn_local",
    )(arrival, weights)


def conv_kernel(block, window, source, ways, kmap, xt_local, rim0, rim1, rim2, rim3, weights_t, occ, resp, stats, xt, g):
    offsets, tile_rows = kmap.shape[0], kmap.shape[2]
    channels = xt_local.shape[1]
    same = same_of(channels)
    lane = lax.broadcasted_iota(I32, (channels, LANES), 1)
    right = lane >= block
    half = jnp.where(lax.broadcasted_iota(I32, (1, LANES), 1) >= block, block, 0)
    rows16 = lax.broadcasted_iota(I32, (LANES, LANES), 0).astype(I16)
    none = jnp.zeros((LANES, LANES), BF16)

    def keep(i, carry):
        xt[i] = xt_local[i]
        return carry

    local_blocks = xt_local.shape[0]
    lax.fori_loop(0, local_blocks, keep, 0, unroll=8)
    for d, part in enumerate((rim0, rim1, rim2, rim3)):
        first = local_blocks + (ways[d] ^ 1) * (part.shape[0] // block)

        def turn(p, carry, part=part, first=first):
            both = jnp.maximum(turn_pair(same, part, p, block), 0.0).astype(BF16)
            xt[first + 2 * p] = both[:, :LANES]
            xt[first + 2 * p + 1] = both[:, LANES:]
            return carry

        lax.fori_loop(0, part.shape[0] // LANES, turn, 0, unroll=8)

    blocks = window // block

    def convolve_window(step, total):
        def pair_of(k, p):
            line = blocks // 2 * step + p
            left_block = source[line, 2 * k]
            right_block = source[line, 2 * k + 1]
            return jnp.where(right, xt[right_block ^ 1], xt[left_block])

        def chooser_of(k, p):
            at = pl.ds(pl.multiple_of(step * window, window) + p * LANES, LANES)
            listed = kmap[k, :, at]
            local = jnp.where(listed < 0, -1, (listed & (block - 1)) + half)
            local = jnp.broadcast_to(local, (LANES, LANES)).astype(I16)
            return jnp.where(rows16 == local, jnp.ones((), BF16), jnp.zeros((), BF16))

        for k in range(offsets):
            for p in range(0, window // LANES, 2):
                to = slice(k * channels, (k + 1) * channels)
                if k == offsets // 2:
                    for q in (p, p + 1):
                        g[to, q * LANES : (q + 1) * LANES] = xt[blocks * step + 2 * q]
                    continue
                if k % LANE_TURN == 0:
                    for q in (p, p + 1):
                        at = pl.ds(pl.multiple_of(step * window, window) + q * LANES, LANES)
                        listed = kmap[k, :, at]
                        index = jnp.broadcast_to((listed & (block - 1)) + half, (channels, LANES)).astype(I16)
                        there = jnp.broadcast_to(listed, (channels, LANES)).astype(I16) >= 0
                        chosen = jnp.where(there, lane_gather(pair_of(k, q), index), jnp.zeros((), BF16))
                        g[to, q * LANES : (q + 1) * LANES] = chosen
                    continue
                pairs = jnp.concatenate((pair_of(k, p), pair_of(k, p + 1)), axis=1)
                chooser = jnp.concatenate(
                    (
                        jnp.concatenate((chooser_of(k, p), none), axis=1),
                        jnp.concatenate((none, chooser_of(k, p + 1)), axis=1),
                    ),
                    axis=0,
                )
                chosen = jnp.dot(pairs, chooser, preferred_element_type=F32).astype(BF16)
                g[to, p * LANES : (p + 2) * LANES] = chosen
        here = pl.ds(pl.multiple_of(step * window, window), window)
        value = jnp.dot(weights_t[...], g[...], preferred_element_type=F32) * occ[:, here]
        resp[:, here] = value
        for p in range(window // LANES):
            total = total + value[:, p * LANES : (p + 1) * LANES]
        return total

    zero = jnp.zeros((channels, LANES), F32)
    total = lax.fori_loop(0, tile_rows // window, convolve_window, zero)
    total = jnp.sum(total, axis=1, keepdims=True)
    number = jnp.sum(occ[...], axis=1, keepdims=True)
    mean = total / jnp.maximum(number, 1.0)

    def spread(p, squares):
        at = pl.ds(pl.multiple_of(p * LANES, LANES), LANES)
        centred = (resp[:, at] - mean) * occ[:, at]
        return squares + centred * centred

    squares = lax.fori_loop(0, tile_rows // LANES, spread, zero, unroll=4)
    squares = jnp.sum(squares, axis=1, keepdims=True)
    columns = jnp.where(lane == 0, total, jnp.where(lane == 1, squares, jnp.broadcast_to(number, (channels, LANES))))
    lines = columns.T
    line = jnp.concatenate((lines[0:1], lines[1:2], lines[2:3]), axis=1)

    def tell(i, carry):
        stats[i] = line
        return carry

    lax.fori_loop(0, stats.shape[0], tell, 0, unroll=8)


def convolve(source, ways, kmap, xt_local, rims, weights_t, occ, block):
    offsets, _, tile_rows = kmap.shape
    local_blocks, channels, _ = xt_local.shape
    window = min(1024, tile_rows)
    ext_blocks = local_blocks + sum(rim.shape[0] for rim in rims) // block
    whole = pl.BlockSpec(memory_space=pltpu.VMEM)
    return pl.pallas_call(
        functools.partial(conv_kernel, block, window),
        in_specs=[pl.BlockSpec(memory_space=pltpu.SMEM)] * 2 + [whole] * 8,
        out_specs=[whole, whole],
        out_shape=[
            jax.ShapeDtypeStruct((channels, tile_rows), F32),
            jax.ShapeDtypeStruct((tile_rows // block, 1, 3 * channels), F32),
        ],
        scratch_shapes=[
            pltpu.VMEM((ext_blocks, channels, LANES), BF16),
            pltpu.VMEM((offsets * channels, window), BF16),
        ],
        compiler_params=pltpu.CompilerParams(vmem_limit_bytes=40 * MIB),
        name="convolve",
    )(source, ways, kmap, xt_local, *rims, weights_t, occ)


def finish_kernel(population, stats, gain, bias, resp, occ, out, stage, sems):
    channels, tile_rows = resp.shape
    total = stats[:, 0, :channels]
    squares = stats[:, 0, channels : 2 * channels]
    number = stats[:, 0, 2 * channels :]
    average = jnp.sum(total, axis=0, keepdims=True) / population
    apart = total / jnp.maximum(number, 1.0) - average
    spread = jnp.sum(squares + number * apart * apart, axis=0, keepdims=True)
    scale = gain[...] / jnp.sqrt(spread / population + 1e-05)
    row = lax.broadcasted_iota(I32, (LANES, channels), 0)
    affine = jnp.where(row == 0, average, jnp.where(row == 1, scale, bias[...])).T
    average, scale, shift = affine[:, 0:1], affine[:, 1:2], affine[:, 2:3]
    count = sems.shape[0]
    part = tile_rows // count
    copies = []
    for c in range(count):

        def turn(p, carry, c=c):
            at = pl.ds(pl.multiple_of(c * part + p * LANES, LANES), LANES)
            value = jnp.maximum((resp[:, at] - average) * scale + shift, 0.0) * occ[:, at]
            stage[at, :] = value.T.astype(BF16)
            return carry

        lax.fori_loop(0, part // LANES, turn, 0, unroll=8)
        here = slice(c * part, (c + 1) * part)
        copies.append(pltpu.make_async_copy(stage.at[here, :], out.at[here, :], sems.at[c]))
        copies[-1].start()
    for copy in copies:
        copy.wait()


def finish(stats, gain, bias, resp, occ, population):
    channels, tile_rows = resp.shape
    whole = pl.BlockSpec(memory_space=pltpu.VMEM)
    return pl.pallas_call(
        functools.partial(finish_kernel, population),
        in_specs=[whole] * 5,
        out_specs=pl.BlockSpec(memory_space=pl.ANY),
        out_shape=jax.ShapeDtypeStruct((tile_rows, channels), BF16),
        scratch_shapes=[pltpu.VMEM((tile_rows, channels), BF16), pltpu.SemaphoreType.DMA((8,))],
        compiler_params=pltpu.CompilerParams(vmem_limit_bytes=16 * MIB),
        name="finish",
    )(stats, gain.reshape(1, channels), bias.reshape(1, channels), resp, occ)


def shards(voxels, owner_tile, rim_blocks, kernel_map, weights, norm_gain, shift_bias):
    devices = lax.axis_size(AXES)
    offsets, tile_rows = kernel_map.shape[1:]
    pair_rows = tile_rows // devices
    block = pair_rows
    channels = voxels.shape[1]

    def swap(value):
        return lax.all_to_all(value, AXES, split_axis=0, concat_axis=0, tiled=True)

    odd_row, odd_col = lax.axis_index("tx") % 2, lax.axis_index("ty") % 2
    ways = jnp.stack((odd_row, 1 - odd_row, 2 + odd_col, 3 - odd_col)).astype(I32)
    outgoing = place(voxels, owner_tile, tile_rows, pair_rows)
    ways, outgoing = lax.optimization_barrier((ways, outgoing))
    arrival = swap(outgoing.reshape(devices, pair_rows, channels)).reshape(tile_rows, channels)
    kmap = kernel_map.transpose(1, 0, 2)
    source = source_blocks(kmap, block)
    picked = pick(arrival, rim_blocks[0], ways, block)
    rims = [None] * len(picked)
    for d, axis, first in ((3, "ty", 1), (1, "tx", 1), (2, "ty", 0), (0, "tx", 0)):
        rims[d] = exchanged(picked[d], axis, first)
    xt, occ, weights_t = turn_local(arrival, weights, block)
    resp, stats = convolve(source, ways, kmap, xt, rims, weights_t, occ, block)
    gathered = swap(stats)
    return finish(gathered, norm_gain, shift_bias, resp, occ, float(voxels.shape[0] * devices))


def solution(mesh):
    return jax.shard_map(
        shards,
        mesh=mesh,
        in_specs=(
            P(AXES, None),
            P(AXES, None),
            P(AXES, None, None),
            P(AXES, None, None),
            P(),
            P(),
            P(),
        ),
        out_specs=P(AXES, None),
        check_vma=False,
    )
```
